128 devices in a mesh: row: 4 (over x), col: 32 (over z, y, core).
Axes of the slice: x: 4, y: 4, z: 4, core: 2. Of those that a mesh axis runs over, the one named last changes fastest.
Arguments:
- frames: bfloat16 [32768, 128], P('col'), may hold values from -3 to 3
- width_class: int32 [32768], P('col'), may hold values from 0 to 3
- start: float32 [16, 32768], P(None, 'col'), may hold values from -6 to 6
Outputs:
- embedding: float32 [16, 32768], P(None, 'col')
- log_degree: float32 [32768], P('col')
The draws below stay inside these ranges and needn't reach their ends.
All inputs are finite; a program needn't handle non-finite values.
Results may differ from the reference program's by a relative error of at most 0.0053.
Values may be sent and summed in bfloat16 or wider, within the bound.
No kernel may reach another device: no remote copies, remote signals or barrier semaphores. Data moves between devices by JAX's collectives and lax.ppermute only.
A program may use at most 128 MiB of HBM per device.

```python
import math
import jax
import jax.numpy as jnp
from jax import lax

F = 128
KV = 16
ITERS = 3
CB = 1024
NTOT = 32768
N_COL = 32


centre_count = 24


spread_low = 0.15


spread_high = 0.36


def draw_frames(key, part):
    key = jax.random.fold_in(key, 11)
    key_centre, key_label, key_spread, key_noise = jax.random.split(key, 4)
    centres = 0.3 * jax.random.normal(key_centre, (centre_count, F), jnp.float32)
    labels = jnp.sort(jax.random.randint(key_label, (NTOT,), 0, centre_count))
    offsets = jax.random.uniform(key_spread, (centre_count,), jnp.float32, 0.0, 1.0)
    ranks = jnp.arange(centre_count, dtype=jnp.float32)
    log_span = math.log(spread_high) - math.log(spread_low)
    spread = jnp.exp(math.log(spread_low) + log_span * (ranks + offsets) / centre_count)
    noise = jax.random.normal(key_noise, (NTOT, F), jnp.float32)
    values = centres[labels] + spread[labels][:, None] * noise
    return jnp.clip(values, -3.0, 3.0).astype(jnp.bfloat16)


def set_ends(array, key, least, high):
    spot = [jax.random.randint(jax.random.fold_in(key, axis), (), 0, length) for axis, length in enumerate(array.shape)]
    widest = array.shape.index(max(array.shape))
    next_to = spot[:widest] + [(spot[widest] + 1) % array.shape[widest]] + spot[widest + 1:]
    return array.at[tuple(spot)].set(least).at[tuple(next_to)].set(high)


def block_scale(key, shape, pieces, least, top_value):
    gain, own = 1.0, jax.random.fold_in(key, 6)
    for position, blocks in pieces:
        draws = jnp.exp(jax.random.uniform(jax.random.fold_in(own, position), (blocks,), jnp.float32, least / len(pieces), top_value / len(pieces)))
        gain = gain * jnp.repeat(draws, shape[position] // blocks).reshape([-1 if axis == position else 1 for axis in range(len(shape))])
    return gain


def normal_values(stream_key, dims, width, limit, pieces=(), kind=jnp.bfloat16):
    loudness = block_scale(stream_key, dims, pieces, -0.22, 0.18) if pieces else 1.0
    values = jax.random.normal(stream_key, dims, jnp.float32) * width * loudness
    return jnp.minimum(jnp.maximum(values, -limit), limit).astype(kind)


def setup_inputs(seed: int = 0) -> dict:
    keys = jax.random.split(jax.random.key(seed), 4)
    return {
        "frames": draw_frames(jax.random.fold_in(keys[3], 71), 0),
        "width_class": set_ends(jax.random.randint(keys[1], (NTOT,), 0, 4), jax.random.fold_in(keys[1], 1), 0, 3).astype(jnp.int32),
        "start": normal_values(keys[2], (KV, NTOT), 1.0, 6.0, ((1, 32),), jnp.float32),
    }


base_width = 2.8
width_growth = 1.3

def kernel_tile(row_frames, row_sq, row_inv, col_frames, col_sq, col_inv):
    products = lax.dot_general(row_frames.astype(jnp.float32), col_frames.astype(jnp.float32), (((1,), (1,)), ((), ())), preferred_element_type=jnp.float32)
    distance = row_sq[:, None] + col_sq[None, :] - 2.0 * products
    return jnp.exp(-(distance * row_inv[:, None]) * col_inv[None, :]).astype(jnp.bfloat16)

def apply_kernel(frames, sq_norm, inv_width, vectors):

    def one_block(block_at):
        start_at = block_at * CB
        row_frames = lax.dynamic_slice_in_dim(frames, start_at, CB, 0)
        row_sq = lax.dynamic_slice_in_dim(sq_norm, start_at, CB, 0)
        row_inv = lax.dynamic_slice_in_dim(inv_width, start_at, CB, 0)
        kernel = kernel_tile(row_frames, row_sq, row_inv, frames, sq_norm, inv_width)
        return lax.dot_general(vectors.astype(jnp.float32), kernel.astype(jnp.float32), (((1,), (1,)), ((), ())), preferred_element_type=jnp.float32)
    stacked = lax.map(one_block, jnp.arange(N_COL, dtype=jnp.int32))
    return jnp.transpose(stacked, (1, 0, 2)).reshape(vectors.shape[0], CB * N_COL)

def reference(frames, width_class, start):
    total_len = CB * N_COL
    sq_norm = lax.optimization_barrier(jnp.sum(jnp.square(frames.astype(jnp.float32)), axis=1))
    inv_width = 1.0 / (base_width * jnp.power(width_growth, width_class.astype(jnp.float32)))
    unit_row = jnp.ones((1, total_len), jnp.bfloat16)
    density = apply_kernel(frames, sq_norm, inv_width, unit_row)[0] / total_len
    inv_density = (1.0 / density).astype(jnp.bfloat16)
    degree = apply_kernel(frames, sq_norm, inv_width, inv_density[None, :])[0] / (total_len * density)
    log_degree = jnp.log(degree)
    weight = 1.0 / (density * jnp.sqrt(degree))
    current = start
    for iteration in range(ITERS):
        scaled = (weight[None, :] * current).astype(jnp.bfloat16)
        projected = weight[None, :] * apply_kernel(frames, sq_norm, inv_width, scaled)
        gram_matrix = jnp.dot(projected, projected.T, precision=lax.Precision.HIGHEST)
        factor = jnp.linalg.cholesky(gram_matrix)
        current = lax.linalg.triangular_solve(factor, projected, left_side=True, lower=True)
    return (math.sqrt(total_len) * current, log_degree)
```

```python
import functools
import math

import jax
import jax.numpy as jnp
from jax import lax
from jax.experimental import pallas as pl
from jax.experimental.pallas import tpu as pltpu
from jax.sharding import Mesh
from jax.sharding import PartitionSpec as P


ITERS = 3
F = 128
CB = 1024
QB = CB // 4
NJ = 2 * CB
NI = 16 * QB
KV = 16
NTOT = 32768
CLS = QB + 4 * KV
PROWS = CLS + 16
base_width = 2.8
width_growth = 1.3
F32 = jnp.float32
BF16 = jnp.bfloat16
VM = pltpu.VMEM
NN = (((1,), (0,)), ((), ()))
NT = (((1,), (1,)), ((), ()))
TN = (((0,), (0,)), ((), ()))


def dot(a, b, dims):
    return lax.dot_general(a, b, dims, preferred_element_type=F32)


def call(kernel, name, outs, args, flops=0, byte_count=0, aliases=None):
    def spec(a):
        if a.dtype == jnp.int32 and a.ndim == 1:
            return pl.BlockSpec(memory_space=pltpu.SMEM)
        return pl.BlockSpec(memory_space=VM)

    return pl.pallas_call(
        kernel,
        out_shape=outs,
        in_specs=[spec(a) for a in args],
        out_specs=jax.tree.map(lambda _: pl.BlockSpec(memory_space=VM), outs),
        compiler_params=pltpu.CompilerParams(vmem_limit_bytes=24 << 20),
        cost_estimate=pl.CostEstimate(flops=flops, bytes_accessed=byte_count, transcendentals=0),
        name=name,
    )(*args)


def sds(shape, dtype=F32):
    return jax.ShapeDtypeStruct(shape, dtype)


def vmem(shape, dtype=F32):
    return pltpu.VMEM(shape, dtype)


def keep(a):
    return pltpu.with_memory_space_constraint(a, VM)


def pack_kernel(pos, frames, classes, start, piece, mine):
    x = pos[0]
    piece[0:QB, :] = frames[pl.ds(pl.multiple_of(x * QB, QB), QB), :]
    quarter = start[:, pl.ds(pl.multiple_of(x * QB, QB), QB)]
    high = quarter.astype(BF16)
    low = (quarter - high.astype(F32)).astype(BF16)
    for h in range(2):
        at = QB + 2 * h * KV
        piece[at : at + KV, :] = high[:, h * 128 : (h + 1) * 128]
        piece[at + KV : at + 2 * KV, :] = low[:, h * 128 : (h + 1) * 128]
    cls = classes[...].astype(F32)
    cls = jnp.concatenate([cls, jnp.zeros_like(cls)], axis=0).astype(BF16)
    piece[CLS:PROWS, :] = cls
    mine[0:CB, :] = frames[...]
    mine[CB : CB + 16, :] = cls


def stack_kernel(a, b, c, d, out):
    for n, ref in enumerate((a, b, c, d)):
        out[n] = ref[...]


def augment(rows, own_first):
    wide = rows.astype(F32)
    half = -0.5 * jnp.sum(wide * wide, axis=1, keepdims=True)
    p1 = half.astype(BF16).astype(F32)
    p2 = (half - p1).astype(BF16).astype(F32)
    p3 = half - p1 - p2
    lane = lax.broadcasted_iota(jnp.int32, (rows.shape[0], 128), 1)
    first = 0 if own_first else 3
    ones = jnp.logical_and(lane >= 3 - first, lane < 6 - first)
    extra = jnp.where(ones, 1.0, 0.0)
    for n, part in enumerate((p1, p2, p3)):
        extra = jnp.where(lane == first + n, part, extra)
    return jnp.concatenate([rows, extra.astype(BF16)], axis=1)


def inverse_width(cls):
    return jnp.exp2(cls * (-math.log2(width_growth))) * (1.0 / base_width)


def make_rows(piece_list, x, aug_j, coef_j, k_ref, row0, sum_j):
    augs, coefs = [], []
    for ref in piece_list:
        augs.append(augment(ref[0:QB, :], True))
        cls = ref[CLS:PROWS, :].astype(F32)
        row = lax.broadcasted_iota(jnp.int32, cls.shape, 0)
        ones = jnp.ones((16, 128), BF16)
        for h in range(2):
            one_row = jnp.where(row == 2 * x + h, cls, 0.0).astype(BF16)
            coefs.append(inverse_width(dot(one_row, ones, TN)[:, :1]))
    aug_i = jnp.concatenate(augs, axis=0)
    coef_i = jnp.concatenate(coefs, axis=0)
    half = 512
    ones_row = jnp.ones((8, half), BF16)
    parts = []
    for n in range(4 * QB // half):
        lo = n * half
        m = dot(aug_i[lo : lo + half], aug_j[...], NT)
        kb = jnp.exp2(m * coef_i[lo : lo + half] * coef_j[...]).astype(BF16)
        k_ref[row0 + lo : row0 + lo + half, :] = kb
        sum_j[...] += dot(ones_row, kb, NN)
        kf = kb.astype(F32)
        acc = kf[:, :128]
        for t in range(1, NJ // 128):
            acc = acc + kf[:, t * 128 : (t + 1) * 128]
        parts.append(acc)
    acc = jnp.concatenate(parts, axis=0)
    ones = jnp.ones((8, 128), BF16)
    a1 = acc.astype(BF16)
    r1 = acc - a1.astype(F32)
    a2 = r1.astype(BF16)
    a3 = (r1 - a2.astype(F32)).astype(BF16)
    return dot(ones, a1, NT) + dot(ones, a2, NT) + dot(ones, a3, NT)


def put_pieces(idx, group, sums, out):
    for n in range(4):
        out[pl.ds(idx[4 * group + n], 1), :] = sums[0:1, n * QB : (n + 1) * QB]


def gen_a_kernel(pos, idx, mine, other, line, aug_j, coef_j, k0, sum_j, sum_i):
    c = pos[1]

    def side(first, second):
        for n, ref in enumerate((first, second)):
            aug_j[n * CB : (n + 1) * CB, :] = augment(ref[0:CB, :], False)
            coef = inverse_width(ref[CB : CB + 16, :].astype(F32)) * (2.0 * math.log2(math.e))
            for r in range(8):
                lo = n * CB + r * 128
                coef_j[:, lo : lo + 128] = coef[r : r + 1, :]

    @pl.when(c == 0)
    def _():
        side(mine, other)

    @pl.when(c != 0)
    def _():
        side(other, mine)

    sum_j[...] = jnp.zeros_like(sum_j)
    sum_i[...] = jnp.zeros_like(sum_i)
    sums = make_rows([line.at[n] for n in range(4)], pos[0], aug_j, coef_j, k0, 0, sum_j)
    put_pieces(idx, 0, sums, sum_i)


def gen_b_kernel(pos, idx, g1, g2, g3, aug_j, coef_j, sum_j_in, sum_i_in, k1, out_j, out_i, sum_j):
    sum_j[...] = sum_j_in[...]
    out_i[...] = sum_i_in[...]
    for g, ref in enumerate((g1, g2, g3)):
        pieces = [ref.at[n] for n in range(4)]
        sums = make_rows(pieces, pos[0], aug_j, coef_j, k1, g * 4 * QB, sum_j)
        put_pieces(idx, g + 1, sums, out_i)
    out_j[...] = sum_j[0:1, :]


def add2_kernel(a0, a1, b0, b1, b2, b3, oa, ob):
    oa[...] = a0[...] + a1[...]
    ob[...] = (b0[...] + b1[...]) + (b2[...] + b3[...])


def spread_pieces(idx, table, scratch):
    for n in range(16):
        scratch[0:1, n * QB : (n + 1) * QB] = table[pl.ds(idx[n], 1), :]


def degree_kernel(idx, k0, k1, j0, j1, j2, j3, i0, i1, i2, i3, dj, di, gj, gi, tab, row):
    sj = ((j0[...] + j1[...]) + (j2[...] + j3[...])) * (1.0 / NTOT)
    si = ((i0[...] + i1[...]) + (i2[...] + i3[...])) * (1.0 / NTOT)
    dj[...] = sj
    di[...] = si
    tab[...] = 1.0 / si
    spread_pieces(idx, tab, row)
    inv_i = jnp.broadcast_to(row[0:1, :], (8, NI)).astype(BF16)
    inv_j = jnp.broadcast_to(1.0 / sj, (8, NJ)).astype(BF16)
    n0 = k0.shape[0]
    g = dot(inv_i[:, :n0], k0[...], NN) + dot(inv_i[:, n0:], k1[...], NN)
    gj[...] = g[0:1, :]
    gi[...] = jnp.zeros_like(gi)
    put_pieces(idx, 0, dot(inv_j, k0[...], NT), gi)
    for n in range(3):
        part = dot(inv_j, k1[n * 4 * QB : (n + 1) * 4 * QB, :], NT)
        put_pieces(idx, n + 1, part, gi)


def split_out(c, y, extra, own, away):
    @pl.when(c == 0)
    def _():
        own[:, :CB] = y[:, :CB]
        away[:, :CB] = y[:, CB:]

    @pl.when(c != 0)
    def _():
        own[:, :CB] = y[:, CB:]
        away[:, :CB] = y[:, :CB]

    if extra is not None:
        own[:, CB:] = extra
        away[:, CB:] = extra


def apply_k(v, k0, k1):
    n0 = k0.shape[0]
    return dot(v[:, :n0], k0[...], NN) + dot(v[:, n0:], k1[...], NN)


def first_kernel(
    pos, idx, k0, k1, line, g1, g2, g3, dj, di, j0, j1, j2, j3, i0, i1, i2, i3,
    own, away, weight_i, weight_own, log_degree, tab, row, vec,
):
    c = pos[1]
    degree_j = ((j0[...] + j1[...]) + (j2[...] + j3[...])) / (NTOT * dj[...])
    degree_i = ((i0[...] + i1[...]) + (i2[...] + i3[...])) / (NTOT * di[...])
    weight_j = 1.0 / (dj[...] * jnp.sqrt(degree_j))
    tab[...] = 1.0 / (di[...] * jnp.sqrt(degree_i))
    spread_pieces(idx, tab, row)
    weight_i[...] = row[...]
    log_j = jnp.log(degree_j)

    @pl.when(c == 0)
    def _():
        weight_own[...] = weight_j[:, :CB]
        log_degree[...] = log_j[:, :CB]

    @pl.when(c != 0)
    def _():
        weight_own[...] = weight_j[:, CB:]
        log_degree[...] = log_j[:, CB:]

    for g, ref in enumerate((line, g1, g2, g3)):
        for n in range(4):
            at = (4 * g + n) * QB
            for h in range(2):
                both = ref[n, QB + 2 * h * KV : QB + 2 * (h + 1) * KV, :].astype(F32)
                part = both[:KV] + both[KV:]
                lo = at + h * 128
                vec[:, lo : lo + 128] = (part * row[0:1, lo : lo + 128]).astype(BF16)
    y = apply_k(vec, k0, k1)
    split_out(c, y, None, own, away)


def next_kernel(pos, idx, k0, k1, weight_i, pieces, own, away, vec, parts):
    c = pos[1]
    for n in range(16):
        at = n * QB
        p = pieces[idx[n]]
        v = p * weight_i[0:1, at : at + QB]
        hi = v.astype(BF16)
        vec[0:KV, at : at + QB] = hi
        vec[KV:, at : at + QB] = (v - hi.astype(F32)).astype(BF16)
        p1 = p.astype(BF16)
        r1 = p - p1.astype(F32)
        p2 = r1.astype(BF16)
        parts[0:KV, at : at + QB] = p1
        parts[KV : 2 * KV, at : at + QB] = p2
        parts[2 * KV :, at : at + QB] = (r1 - p2.astype(F32)).astype(BF16)
    s = dot(parts[...], parts[...], NT)
    rows = s[0:KV] + s[KV : 2 * KV] + s[2 * KV :]
    gram = rows[:, 0:KV] + rows[:, KV : 2 * KV] + rows[:, 2 * KV :]
    gram = jnp.concatenate([gram, jnp.zeros((KV, 128 - KV), F32)], axis=1)
    y2 = apply_k(vec, k0, k1)
    split_out(c, y2[0:KV] + y2[KV:], gram, own, away)


def core_sum_kernel(pos, own, away, q0, q1, q2, q3):
    x = pos[0]
    total = own[...] + away[...]
    width = own.shape[1]
    q0_refs = (q0, q1, q2, q3)
    for t in range(4):
        for d in range(4):

            @pl.when((x + d) % 4 == t)
            def _(t=t, d=d):
                q0_refs[d][:, :QB] = total[:, t * QB : (t + 1) * QB]

    if width > CB:
        for ref in q0_refs:
            ref[:, QB:] = total[:, CB:]


def core_add_kernel(own, away, out):
    out[...] = own[...] + away[...]


def eliminate(gram, y):
    row = lax.broadcasted_iota(jnp.int32, (KV, 1), 0)
    for k in range(KV):
        scale = 1.0 / jnp.sqrt(gram[k : k + 1, k : k + 1])
        col = jnp.where(row > k, gram[:, k : k + 1], 0.0) * scale
        g_row = gram[k : k + 1, :] * scale
        y_row = y[k : k + 1, :] * scale
        gram = gram - col * g_row
        y = jnp.where(row == k, y_row, y - col * y_row)
    return y


def quarter_of(ref, x):
    return ref[0:1, pl.ds(pl.multiple_of(x * QB, QB), QB)]


def project_kernel(with_gram, pos, weight_own, q0, q1, q2, q3, out):
    total = (q0[...] + q1[...]) + (q2[...] + q3[...])
    y = total[:, :QB]
    if with_gram:
        y = eliminate(total[:, QB:], y)
    p = y * quarter_of(weight_own, pos[0])
    for n in range(16):
        out[n] = p


def last_kernel(weight_own, q0, q1, q2, q3, proj, grams):
    total = (q0[...] + q1[...]) + (q2[...] + q3[...])
    y = eliminate(total[:, CB:], total[:, :CB])
    p = y * weight_own[...]
    proj[...] = p
    gram = lax.dot_general(p, p, NT, precision=lax.Precision.HIGHEST, preferred_element_type=F32)
    gram = jnp.concatenate([gram, jnp.zeros((KV, 128 - KV), F32)], axis=1)
    for n in range(32):
        grams[n] = gram


def finish_kernel(proj, grams, out):
    gram = grams[0]
    for n in range(1, 32):
        gram = gram + grams[n]
    out[...] = eliminate(gram, proj[...]) * math.sqrt(NTOT)


def device_number(x, z, y, c):
    return (((x % 4) * 4 + z % 4) * 4 + y % 4) * 2 + c % 2


def shift(v, source):
    pairs = [
        (device_number(*source(x, z, y, c)), device_number(x, z, y, c))
        for x in range(4)
        for z in range(4)
        for y in range(4)
        for c in range(2)
    ]
    return lax.ppermute(v, ("x", "z", "y", "c"), pairs)


def from_line(v, d, second=False):
    def source(x, z, y, c):
        along_y = (c == 0) != second
        return (x, z, y + d, c) if along_y else (x, z + d, y, c)

    return shift(v, source)


def from_x(v, d):
    return shift(v, lambda x, z, y, c: (x + d, z, y, c))


def from_y(v, d):
    return shift(v, lambda x, z, y, c: (x, z, y + d, c))


def from_z(v, d):
    return shift(v, lambda x, z, y, c: (x, z + d, y, c))


def from_core(v):
    return shift(v, lambda x, z, y, c: (x, z, y, c + 1))


def body(frames, width_class, start):
    x, z, y, c = (lax.axis_index(a) for a in ("x", "z", "y", "c"))
    pos = jnp.stack([x, c]).astype(jnp.int32)
    second, first = jnp.arange(16, dtype=jnp.int32) // 4, jnp.arange(16, dtype=jnp.int32) % 4
    piece_y = (y + jnp.where(c == 0, first, second)) % 4
    piece_z = (z + jnp.where(c == 0, second, first)) % 4
    idx = (piece_y * 4 + piece_z).astype(jnp.int32)

    piece, mine = call(
        pack_kernel,
        "pack",
        [sds((PROWS, F), BF16), sds((CB + 16, F), BF16)],
        (pos, frames, width_class.reshape(8, 128), start),
    )
    line = [piece] + [from_line(piece, d) for d in (1, 2, 3)]
    other = from_core(mine)
    line = call(stack_kernel, "stack", sds((4, PROWS, F), BF16), line)
    groups = [from_line(line, d, True) for d in (1, 2, 3)]
    aug_j, coef_j, k0, sum_j, sum_i = call(
        gen_a_kernel,
        "rows_a",
        [
            sds((NJ, 2 * F), BF16),
            sds((1, NJ)),
            vmem((4 * QB, NJ), BF16),
            sds((8, NJ)),
            sds((16, QB)),
        ],
        (pos, idx, mine, other, line),
        flops=4 * QB * NJ * 512,
    )
    k1, sum_j, sum_i = pl.pallas_call(
        gen_b_kernel,
        out_shape=[vmem((12 * QB, NJ), BF16), sds((1, NJ)), sds((16, QB))],
        in_specs=[pl.BlockSpec(memory_space=pltpu.SMEM)] * 2 + [pl.BlockSpec(memory_space=VM)] * 7,
        out_specs=[pl.BlockSpec(memory_space=VM)] * 3,
        scratch_shapes=[pltpu.VMEM((8, NJ), F32)],
        compiler_params=pltpu.CompilerParams(vmem_limit_bytes=24 << 20),
        name="rows_b",
    )(pos, idx, *groups, aug_j, coef_j, sum_j, sum_i)

    def sum_sides(on_j, on_i, step):
        j_terms = [on_j, from_core(on_j)]
        i_terms = [on_i] + [from_y(on_i, d) for d in (1, 2, 3)]
        on_j, on_i = call(
            add2_kernel, step, [sds((1, NJ)), sds((16, QB))], (*j_terms, *i_terms)
        )
        j_terms = [on_j] + [from_x(on_j, d) for d in (1, 2, 3)]
        i_terms = [on_i] + [from_z(on_i, d) for d in (1, 2, 3)]
        return (*j_terms, *i_terms)

    def call_big(kernel, name, outs, args, scratch):
        specs = [
            pl.BlockSpec(memory_space=pltpu.SMEM if a.dtype == jnp.int32 else VM) for a in args
        ]
        return pl.pallas_call(
            kernel,
            out_shape=outs,
            in_specs=specs,
            out_specs=[pl.BlockSpec(memory_space=VM)] * len(outs),
            scratch_shapes=scratch,
            compiler_params=pltpu.CompilerParams(vmem_limit_bytes=24 << 20),
            name=name,
        )(*args)

    terms = sum_sides(sum_j, sum_i, "density_sum")
    table, row = pltpu.VMEM((16, QB), F32), pltpu.VMEM((1, NI), F32)
    dens_j, dens_i, sum_j, sum_i = call_big(
        degree_kernel,
        "degree",
        [sds((1, NJ)), sds((16, QB)), sds((1, NJ)), sds((16, QB))],
        (idx, keep(k0), keep(k1), *terms),
        [table, row],
    )
    terms = sum_sides(sum_j, sum_i, "degree_sum")
    own, away, weight_i, weight_own, log_degree = call_big(
        first_kernel,
        "first",
        [sds((KV, CB)), sds((KV, CB)), sds((1, NI)), sds((1, CB)), sds((1, CB))],
        (pos, idx, keep(k0), keep(k1), line, *groups, dens_j, dens_i, *terms),
        [table, row, pltpu.VMEM((KV, NI), BF16)],
    )
    for iteration in range(1, ITERS):
        width = own.shape[1] - CB + QB
        quarters = call(
            core_sum_kernel, f"core_sum{iteration}", [sds((KV, width))] * 4, (pos, own, from_core(away))
        )
        quarters = [quarters[0]] + [from_x(quarters[4 - d], d) for d in (1, 2, 3)]
        pieces = call(
            functools.partial(project_kernel, iteration > 1),
            f"project{iteration}",
            sds((16, KV, QB)),
            (pos, weight_own, *quarters),
        )
        pieces = lax.all_to_all(pieces, ("y", "z"), 0, 0)
        own, away = call_big(
            next_kernel,
            f"next{iteration}",
            [sds((KV, CB + 128)), sds((KV, CB + 128))],
            (pos, idx, keep(k0), keep(k1), weight_i, pieces),
            [pltpu.VMEM((2 * KV, NI), BF16), pltpu.VMEM((3 * KV, NI), BF16)],
        )
    total = call(core_add_kernel, "core_add", sds((KV, CB + 128)), (own, from_core(away)))
    totals = [total] + [from_x(total, d) for d in (1, 2, 3)]
    proj, grams = call(
        last_kernel, "last", [sds((KV, CB)), sds((32, KV, 128))], (weight_own, *totals)
    )
    grams = lax.all_to_all(grams, ("z", "y", "c"), 0, 0)
    embedding = call(finish_kernel, "finish", sds((KV, CB)), (proj, grams))
    return embedding, log_degree.reshape(CB)


def solution(mesh):
    grid = Mesh(mesh.devices.reshape(4, 4, 4, 2), ("x", "z", "y", "c"))
    col = ("z", "y", "c")
    in_specs = (P(col, None), P(col), P(None, col))
    out_specs = (P(None, col), P(col))
    return jax.shard_map(body, mesh=grid, in_specs=in_specs, out_specs=out_specs, check_vma=False)
```

```python
import functools
import math

import jax
import jax.numpy as jnp
from jax import lax
from jax.experimental import pallas as pl
from jax.experimental.pallas import tpu as pltpu
from jax.sharding import Mesh
from jax.sharding import PartitionSpec as P


ITERS = 3
F = 128
CB = 1024
QB = CB // 4
NJ = 2 * CB
NI = 16 * QB
KV = 16
NTOT = 32768
GROUPS = (0, 1, 3, 2)
LAST_GROUP = GROUPS[-1]
CLS = QB + 4 * KV
PROWS = CLS + 16
base_width = 2.8
width_growth = 1.3
F32 = jnp.float32
BF16 = jnp.bfloat16
VM = pltpu.VMEM
NN = (((1,), (0,)), ((), ()))
NT = (((1,), (1,)), ((), ()))
TN = (((0,), (0,)), ((), ()))


def dot(a, b, dims):
    return lax.dot_general(a, b, dims, preferred_element_type=F32)


def call(kernel, name, outs, args, flops=0, scratch=(), far=()):
    def spec(n, a):
        if a.dtype == jnp.int32 and a.ndim == 1:
            return pl.BlockSpec(memory_space=pltpu.SMEM)
        return pl.BlockSpec(memory_space=pltpu.HBM if n in far else VM)

    return pl.pallas_call(
        kernel,
        out_shape=outs,
        in_specs=[spec(n, a) for n, a in enumerate(args)],
        out_specs=jax.tree.map(lambda _: pl.BlockSpec(memory_space=VM), outs),
        scratch_shapes=scratch,
        compiler_params=pltpu.CompilerParams(vmem_limit_bytes=24 << 20),
        cost_estimate=pl.CostEstimate(flops=flops, bytes_accessed=0, transcendentals=0),
        name=name,
    )(*args)


def sds(shape, dtype=F32):
    return jax.ShapeDtypeStruct(shape, dtype)


def vmem(shape, dtype=F32):
    return pltpu.VMEM(shape, dtype)


def keep(a):
    return pltpu.with_memory_space_constraint(a, VM)


def pack_kernel(pos, frames, classes, start, piece, cls_out, quarter, own_classes, sems):
    at = pl.multiple_of(pos[0] * QB, QB)
    copies = (
        pltpu.make_async_copy(frames.at[pl.ds(at, QB), :], piece.at[0:QB, :], sems.at[0]),
        pltpu.make_async_copy(start.at[:, pl.ds(at, QB)], quarter, sems.at[1]),
        pltpu.make_async_copy(classes, own_classes, sems.at[2]),
    )
    for copy in copies:
        copy.start()
    for copy in copies:
        copy.wait()
    cls = own_classes[...].astype(F32)
    cls = jnp.concatenate([cls, jnp.zeros_like(cls)], axis=0).astype(BF16)
    piece[CLS:PROWS, :] = cls
    cls_out[...] = cls
    high = quarter[...].astype(BF16)
    low = (quarter[...] - high.astype(F32)).astype(BF16)
    for h in range(2):
        at = QB + 2 * h * KV
        piece[at : at + KV, :] = high[:, h * 128 : (h + 1) * 128]
        piece[at + KV : at + 2 * KV, :] = low[:, h * 128 : (h + 1) * 128]


def stack_kernel(a, b, c, d, ready, out):
    del ready
    for n, ref in enumerate((a, b, c, d)):
        out[n] = ref[...]


def augment(rows, own_first):
    wide = rows.astype(F32)
    half = -0.5 * jnp.sum(wide * wide, axis=1, keepdims=True)
    p1 = half.astype(BF16).astype(F32)
    p2 = (half - p1).astype(BF16).astype(F32)
    p3 = half - p1 - p2
    lane = lax.broadcasted_iota(jnp.int32, (rows.shape[0], 128), 1)
    first = 0 if own_first else 3
    ones = jnp.logical_and(lane >= 3 - first, lane < 6 - first)
    extra = jnp.where(ones, 1.0, 0.0)
    for n, part in enumerate((p1, p2, p3)):
        extra = jnp.where(lane == first + n, part, extra)
    return jnp.concatenate([rows, extra.astype(BF16)], axis=1)


def inverse_width(cls):
    return jnp.exp2(cls * (-math.log2(width_growth))) * (1.0 / base_width)


def side_kernel(pos, mine, mine_cls, other, other_cls, aug_j, coef_j):
    c = pos[1]

    def side(blocks):
        for n, (rows, cls) in enumerate(blocks):
            aug_j[n * CB : (n + 1) * CB, :] = augment(rows[...], False)
            coef = inverse_width(cls[...].astype(F32)) * (2.0 * math.log2(math.e))
            for r in range(8):
                lo = n * CB + r * 128
                coef_j[:, lo : lo + 128] = coef[r : r + 1, :]

    @pl.when(c == 0)
    def _():
        side(((mine, mine_cls), (other, other_cls)))

    @pl.when(c != 0)
    def _():
        side(((other, other_cls), (mine, mine_cls)))


def spread(sum_j, out):
    for n in range(128):
        lo = n % 2 * CB + n // 2 % 4 * QB
        out[n] = sum_j[:, lo : lo + QB]


def rows_kernel(group, pos, pieces, aug_j, coef_j, *refs):
    k_ref, out, sum_j = refs[-3:]
    x = pos[0]
    sum_j[...] = jnp.zeros_like(sum_j) if group == 0 else refs[0][...]
    augs, coefs = [], []
    row = lax.broadcasted_iota(jnp.int32, (16, 128), 0)
    ones = jnp.ones((16, 128), BF16)
    for n in range(4):
        augs.append(augment(pieces[n, 0:QB, :], True))
        cls = pieces[n, CLS:PROWS, :].astype(F32)
        for h in range(2):
            one_row = jnp.where(row == 2 * x + h, cls, 0.0).astype(BF16)
            coefs.append(inverse_width(dot(one_row, ones, TN)[:, :1]))
    aug_i = jnp.concatenate(augs, axis=0)
    coef_i = jnp.concatenate(coefs, axis=0)
    half = 512
    ones_row = jnp.ones((8, half), BF16)
    for lo in range(0, 4 * QB, half):
        m = dot(aug_i[lo : lo + half], aug_j[...], NT)
        kb = jnp.exp2(m * coef_i[lo : lo + half] * coef_j[...]).astype(BF16)
        k_ref[lo : lo + half, :] = kb
        sum_j[...] += dot(ones_row, kb, NN)[0:1]
    if group == LAST_GROUP:
        spread(sum_j, out)
    else:
        out[...] = sum_j[...]


def side_i(pos, table, row):
    for n in range(16):
        at = pos[2 + n] * 8
        terms = [table[at + k] for k in range(8)]
        while len(terms) > 1:
            terms = [a + b for a, b in zip(terms[::2], terms[1::2])]
        row[:, n * QB : (n + 1) * QB] = terms[0]


def apply_k(v, ks, columns=slice(None)):
    n0 = NI // len(ks)
    terms = [dot(v[:, n * n0 : (n + 1) * n0], k[:, columns], NN) for n, k in enumerate(ks)]
    return (terms[0] + terms[1]) + (terms[2] + terms[3])


def degree_kernel(pos, k0, k1, k2, k3, table, dens_i, out, sum_j):
    side_i(pos, table, dens_i)
    dens_i[...] = dens_i[...] * (1.0 / NTOT)
    inverse = jnp.broadcast_to(1.0 / dens_i[...], (8, NI)).astype(BF16)
    sum_j[...] = apply_k(inverse, (k0, k1, k2, k3))[0:1]
    spread(sum_j, out)


def half(c):
    return pl.ds(pl.multiple_of(c * CB, CB), CB)


def first_kernel(
    pos, k0, k1, k2, k3, g0, g1, g2, g3, dens_i, table,
    vec, weight_i, weight_log, away, row,
):
    side_i(pos, table, row)
    row[...] = row[...] / (NTOT * dens_i[...])
    weight_i[...] = 1.0 / (dens_i[...] * jnp.sqrt(row[...]))
    weight_log[0:1, :] = weight_i[:, :QB]
    weight_log[1:2, :] = jnp.log(row[:, :QB])
    weight_log[2:, :] = jnp.zeros((6, QB), F32)
    for g, ref in enumerate((g0, g1, g2, g3)):
        for n in range(4):
            at = (4 * g + n) * QB
            for h in range(2):
                both = ref[n, QB + 2 * h * KV : QB + 2 * (h + 1) * KV, :].astype(F32)
                lo = at + h * 128
                part = (both[:KV] + both[KV:]) * weight_i[:, lo : lo + 128]
                vec[:, lo : lo + 128] = part.astype(BF16)
    away[...] = apply_k(vec, (k0, k1, k2, k3), half(1 - pos[1]))


def own_kernel(pos, k0, k1, k2, k3, vec, own):
    y = apply_k(vec, (k0, k1, k2, k3), half(pos[1]))
    if vec.shape[0] == 2 * KV:
        y = y[:KV] + y[KV:]
    own[...] = y


def next_kernel(pos, k0, k1, k2, k3, weight_i, pieces, vec, gram, away, parts):
    for n in range(16):
        at = n * QB
        p = pieces[pos[2 + n]]
        v = p * weight_i[0:1, at : at + QB]
        hi = v.astype(BF16)
        vec[0:KV, at : at + QB] = hi
        vec[KV:, at : at + QB] = (v - hi.astype(F32)).astype(BF16)
        p1 = p.astype(BF16)
        r1 = p - p1.astype(F32)
        p2 = r1.astype(BF16)
        parts[0:KV, at : at + QB] = p1
        parts[KV : 2 * KV, at : at + QB] = p2
        parts[2 * KV :, at : at + QB] = (r1 - p2.astype(F32)).astype(BF16)
    s = dot(parts[...], parts[...], NT)
    rows = s[0:KV] + s[KV : 2 * KV] + s[2 * KV :]
    square = rows[:, 0:KV] + rows[:, KV : 2 * KV] + rows[:, 2 * KV :]
    square = jnp.concatenate([square, jnp.zeros((KV, 128 - KV), F32)], axis=1)
    gram[...] = square
    y2 = apply_k(vec, (k0, k1, k2, k3), half(1 - pos[1]))
    away[:, :CB] = y2[0:KV] + y2[KV:]
    away[:, CB:] = square


def core_sum_kernel(pos, own, away, *refs):
    outs = refs[-4:]
    x = pos[0]
    total = own[...] + away[:, :CB]
    for t in range(4):
        for d in range(4):

            @pl.when((x + d) % 4 == t)
            def _(t=t, d=d):
                outs[d][:KV, :QB] = total[:, t * QB : (t + 1) * QB]

    if away.shape[1] > CB:
        gram = refs[0][...] + away[:, CB:]
        for ref in outs:
            ref[:, QB:] = gram
    else:
        for ref in outs:
            ref[KV:, :] = refs[0][...]


def core_add_kernel(own, away, gram, out):
    out[:, :CB] = own[...] + away[:, :CB]
    out[:, CB:] = gram[...] + away[:, CB:]


def eliminate(gram, y):
    row = lax.broadcasted_iota(jnp.int32, (KV, 1), 0)
    pivots = jnp.zeros((KV, 1), F32)
    for k in range(KV):
        pivot = gram[k : k + 1, k : k + 1]
        ratio = jnp.where(row > k, gram[:, k : k + 1] * (1.0 / pivot), 0.0)
        pivots = jnp.where(row == k, pivot, pivots)
        gram, y = gram - ratio * gram[k : k + 1, :], y - ratio * y[k : k + 1, :]
    return y * (1.0 / jnp.sqrt(pivots))


def project_first_kernel(pos, weight_log, q0, q1, q2, q3, out, weight_own, log_degree):
    y = (q0[:KV] + q1[:KV]) + (q2[:KV] + q3[:KV])
    p = y * weight_log[0:1, :]
    for n in range(16):
        out[n] = p
    for d, ref in enumerate((q0, q1, q2, q3)):
        at = pl.ds(pl.multiple_of((pos[0] + d) % 4 * QB, QB), QB)
        weight_own[:, at] = ref[KV : KV + 1, :]
        log_degree[:, at] = ref[KV + 1 : KV + 2, :]


def project_kernel(weight_log, q0, q1, q2, q3, out):
    total = (q0[...] + q1[...]) + (q2[...] + q3[...])
    p = eliminate(total[:, QB:], total[:, :QB]) * weight_log[0:1, :]
    for n in range(16):
        out[n] = p


def last_kernel(weight_own, q0, q1, q2, q3, proj, grams):
    total = (q0[...] + q1[...]) + (q2[...] + q3[...])
    y = eliminate(total[:, CB:], total[:, :CB])
    p = y * weight_own[...]
    proj[...] = p
    gram = lax.dot_general(p, p, NT, precision=lax.Precision.HIGHEST, preferred_element_type=F32)
    gram = jnp.concatenate([gram, jnp.zeros((KV, 128 - KV), F32)], axis=1)
    for n in range(32):
        grams[n] = gram


def finish_kernel(proj, grams, out):
    gram = grams[0]
    for n in range(1, 32):
        gram = gram + grams[n]
    out[...] = eliminate(gram, proj[...]) * math.sqrt(NTOT)


def device_number(x, z, y, c):
    return (((x % 4) * 4 + z % 4) * 4 + y % 4) * 2 + c % 2


def shift(v, source):
    pairs = [
        (device_number(*source(x, z, y, c)), device_number(x, z, y, c))
        for x in range(4)
        for z in range(4)
        for y in range(4)
        for c in range(2)
    ]
    return lax.ppermute(v, ("x", "z", "y", "c"), pairs)


def from_line(v, d, second=False):
    def source(x, z, y, c):
        along_y = (c == 0) != second
        return (x, z, y + d, c) if along_y else (x, z + d, y, c)

    return shift(v, source)


def from_x(v, d):
    return shift(v, lambda x, z, y, c: (x + d, z, y, c))


def from_core(v):
    return shift(v, lambda x, z, y, c: (x, z, y, c + 1))


def body(frames, width_class, start):
    x, z, y, c = (lax.axis_index(a) for a in ("x", "z", "y", "c"))
    second, first = jnp.arange(16, dtype=jnp.int32) // 4, jnp.arange(16, dtype=jnp.int32) % 4
    piece_y = (y + jnp.where(c == 0, first, second)) % 4
    piece_z = (z + jnp.where(c == 0, second, first)) % 4
    pos = jnp.concatenate([jnp.stack([x, c]), piece_y * 4 + piece_z]).astype(jnp.int32)

    classes = width_class.reshape(8, 128)
    piece, cls = call(
        pack_kernel,
        "pack",
        [sds((PROWS, F), BF16), sds((16, 128), BF16)],
        (pos, *(pltpu.with_memory_space_constraint(a, pltpu.HBM) for a in (frames, classes, start))),
        scratch=[
            pltpu.VMEM((KV, QB), F32),
            pltpu.VMEM((8, 128), jnp.int32),
            pltpu.SemaphoreType.DMA((3,)),
        ],
        far=(1, 2, 3),
    )
    line = [piece] + [from_line(piece, d) for d in (1, 2, 3)]
    aug_j, coef_j = call(
        side_kernel,
        "side",
        [sds((NJ, 2 * F), BF16), sds((1, NJ))],
        (pos, frames, cls, from_core(frames), from_core(cls)),
        flops=NJ * 4000,
    )
    line = call(stack_kernel, "stack", sds((4, PROWS, F), BF16), (*line, coef_j))
    groups = [line] + [from_line(line, d, True) for d in (1, 2, 3)]
    ks, sums = [None] * 4, ()
    for g in GROUPS:
        ks[g], sums = call(
            functools.partial(rows_kernel, g),
            f"rows{g}",
            [vmem((4 * QB, NJ), BF16), sds((128, 1, QB) if g == LAST_GROUP else (1, NJ))],
            (pos, groups[g], aug_j, coef_j) + (() if g == 0 else (sums,)),
            flops=4 * QB * NJ * 1024,
            scratch=[pltpu.VMEM((1, NJ), F32)],
        )

    def tile():
        return [keep(k) for k in ks]

    everyone = ("y", "z", "x", "c")
    dens_i, table = call(
        degree_kernel,
        "degree",
        [sds((1, NI)), sds((128, 1, QB))],
        (pos, *tile(), lax.all_to_all(sums, everyone, 0, 0)),
        scratch=[pltpu.VMEM((1, NJ), F32)],
    )
    vec, weight_i, weight_log, away = call(
        first_kernel,
        "first",
        [sds((KV, NI), BF16), sds((1, NI)), sds((8, QB)), sds((KV, CB))],
        (pos, *tile(), *groups, dens_i, lax.all_to_all(table, everyone, 0, 0)),
        scratch=[pltpu.VMEM((1, NI), F32)],
    )
    flops = 2 * NI * CB * 256

    def own_half(iteration):
        return call(own_kernel, f"own{iteration}", sds((KV, CB)), (pos, *tile(), vec), flops=flops)

    for iteration in range(1, ITERS):
        shape = (KV + 8, QB) if iteration == 1 else (KV, QB + 128)
        quarters = call(
            core_sum_kernel,
            f"core_sum{iteration}",
            [sds(shape)] * 4,
            (pos, own_half(iteration), from_core(away), weight_log if iteration == 1 else square),
        )
        quarters = [quarters[0]] + [from_x(quarters[4 - d], d) for d in (1, 2, 3)]
        if iteration == 1:
            pieces, weight_own, log_degree = call(
                project_first_kernel,
                "project1",
                [sds((16, KV, QB)), sds((1, CB)), sds((1, CB))],
                (pos, weight_log, *quarters),
            )
        else:
            pieces = call(
                project_kernel,
                f"project{iteration}",
                sds((16, KV, QB)),
                (weight_log, *quarters),
            )
        pieces = lax.all_to_all(pieces, ("y", "z"), 0, 0)
        vec, square, away = call(
            next_kernel,
            f"next{iteration}",
            [sds((2 * KV, NI), BF16), sds((KV, 128)), sds((KV, CB + 128))],
            (pos, *tile(), weight_i, pieces),
            scratch=[pltpu.VMEM((3 * KV, NI), BF16)],
        )
    total = call(
        core_add_kernel,
        "core_add",
        sds((KV, CB + 128)),
        (own_half(ITERS), from_core(away), square),
    )
    totals = [total] + [from_x(total, d) for d in (1, 2, 3)]
    proj, grams = call(
        last_kernel, "last", [sds((KV, CB)), sds((32, KV, 128))], (weight_own, *totals)
    )
    grams = lax.all_to_all(grams, ("z", "y", "c"), 0, 0)
    embedding = call(finish_kernel, "finish", sds((KV, CB)), (proj, grams))
    return embedding, log_degree.reshape(CB)


def solution(mesh):
    grid = Mesh(mesh.devices.reshape(4, 4, 4, 2), ("x", "z", "y", "c"))
    col = ("z", "y", "c")
    in_specs = (P(col, None), P(col), P(None, col))
    out_specs = (P(None, col), P(col))
    return jax.shard_map(body, mesh=grid, in_specs=in_specs, out_specs=out_specs, check_vma=False)
```

```python
import functools
import math

import jax
import jax.numpy as jnp
from jax import lax
from jax.experimental import pallas as pl
from jax.experimental.pallas import tpu as pltpu
from jax.sharding import Mesh
from jax.sharding import PartitionSpec as P


ITERS = 3
F = 128
CB = 1024
QB = CB // 4
NJ = 2 * CB
NI = 16 * QB
KV = 16
NTOT = 32768
GROUPS = (0, 1, 3, 2)
LAST_GROUP = GROUPS[-1]
CLS = QB + 4 * KV
PROWS = CLS + 16
base_width = 2.8
width_growth = 1.3
F32 = jnp.float32
BF16 = jnp.bfloat16
VM = pltpu.VMEM
NN = (((1,), (0,)), ((), ()))
NT = (((1,), (1,)), ((), ()))
TN = (((0,), (0,)), ((), ()))


def dot(a, b, dims):
    return lax.dot_general(a, b, dims, preferred_element_type=F32)


def call(kernel, name, outs, args, flops=0, scratch=(), far=()):
    def spec(n, a):
        if a.dtype == jnp.int32 and a.ndim == 1:
            return pl.BlockSpec(memory_space=pltpu.SMEM)
        return pl.BlockSpec(memory_space=pltpu.HBM if n in far else VM)

    return pl.pallas_call(
        kernel,
        out_shape=outs,
        in_specs=[spec(n, a) for n, a in enumerate(args)],
        out_specs=jax.tree.map(lambda _: pl.BlockSpec(memory_space=VM), outs),
        scratch_shapes=scratch,
        compiler_params=pltpu.CompilerParams(vmem_limit_bytes=24 << 20),
        cost_estimate=pl.CostEstimate(flops=flops, bytes_accessed=0, transcendentals=0),
        name=name,
    )(*args)


def sds(shape, dtype=F32):
    return jax.ShapeDtypeStruct(shape, dtype)


def vmem(shape, dtype=F32):
    return pltpu.VMEM(shape, dtype)


def keep(a):
    return pltpu.with_memory_space_constraint(a, VM)


def pack_kernel(pos, frames, classes, start, piece, cls_out, mine, quarter, own_classes, sems):
    at = pl.multiple_of(pos[0] * QB, QB)
    copies = (
        pltpu.make_async_copy(frames.at[pl.ds(at, QB), :], piece.at[0:QB, :], sems.at[0]),
        pltpu.make_async_copy(start.at[:, pl.ds(at, QB)], quarter, sems.at[1]),
        pltpu.make_async_copy(classes, own_classes, sems.at[2]),
        pltpu.make_async_copy(frames, mine, sems.at[3]),
    )
    for copy in copies:
        copy.start()
    for copy in copies:
        copy.wait()
    cls = own_classes[...].astype(F32)
    cls = jnp.concatenate([cls, jnp.zeros_like(cls)], axis=0).astype(BF16)
    piece[CLS:PROWS, :] = cls
    cls_out[...] = cls
    high = quarter[...].astype(BF16)
    low = (quarter[...] - high.astype(F32)).astype(BF16)
    for h in range(2):
        at = QB + 2 * h * KV
        piece[at : at + KV, :] = high[:, h * 128 : (h + 1) * 128]
        piece[at + KV : at + 2 * KV, :] = low[:, h * 128 : (h + 1) * 128]


def stack_kernel(a, b, c, d, ready, out):
    del ready
    for n, ref in enumerate((a, b, c, d)):
        out[n] = ref[...]


def augment(rows, own_first):
    wide = rows.astype(F32)
    half = -0.5 * jnp.sum(wide * wide, axis=1, keepdims=True)
    p1 = half.astype(BF16).astype(F32)
    p2 = (half - p1).astype(BF16).astype(F32)
    p3 = half - p1 - p2
    lane = lax.broadcasted_iota(jnp.int32, (rows.shape[0], 128), 1)
    first = 0 if own_first else 3
    ones = jnp.logical_and(lane >= 3 - first, lane < 6 - first)
    extra = jnp.where(ones, 1.0, 0.0)
    for n, part in enumerate((p1, p2, p3)):
        extra = jnp.where(lane == first + n, part, extra)
    return jnp.concatenate([rows, extra.astype(BF16)], axis=1)


def inverse_width(cls):
    return jnp.exp2(cls * (-math.log2(width_growth))) * (1.0 / base_width)


def side_kernel(pos, mine, mine_cls, other, other_cls, aug_j, coef_j):
    c = pos[1]

    def side(blocks):
        for n, (rows, cls) in enumerate(blocks):
            aug_j[n * CB : (n + 1) * CB, :] = augment(rows[...], False)
            coef = inverse_width(cls[...].astype(F32)) * (2.0 * math.log2(math.e))
            for r in range(8):
                lo = n * CB + r * 128
                coef_j[:, lo : lo + 128] = coef[r : r + 1, :]

    @pl.when(c == 0)
    def _():
        side(((mine, mine_cls), (other, other_cls)))

    @pl.when(c != 0)
    def _():
        side(((other, other_cls), (mine, mine_cls)))


def spread(sum_j, out):
    for n in range(128):
        lo = n % 2 * CB + n // 2 % 4 * QB
        out[n] = sum_j[:, lo : lo + QB]


def rows_kernel(group, pos, pieces, aug_j, coef_j, *refs):
    k_ref, out = refs[-2:]
    x = pos[0]
    augs, coefs = [], []
    row = lax.broadcasted_iota(jnp.int32, (16, 128), 0)
    ones = jnp.ones((16, 128), BF16)
    for n in range(4):
        augs.append(augment(pieces[n, 0:QB, :], True))
        cls = pieces[n, CLS:PROWS, :].astype(F32)
        for h in range(2):
            one_row = jnp.where(row == 2 * x + h, cls, 0.0).astype(BF16)
            coefs.append(inverse_width(dot(one_row, ones, TN)[:, :1]))
    half = 512
    total = jnp.zeros((8, NJ), F32) if group == 0 else refs[0][...]
    for n in range(2):
        aug_i = jnp.concatenate(augs[2 * n : 2 * n + 2], axis=0)
        coef_i = jnp.concatenate(coefs[4 * n : 4 * n + 4], axis=0)
        e = jnp.exp2(dot(aug_i, aug_j[...], NT) * coef_i * coef_j[...])
        k_ref[n * half : (n + 1) * half, :] = e.astype(BF16)
        total = total + jnp.sum(e.reshape(half // 8, 8, NJ), axis=0)
    if group == LAST_GROUP:
        spread(jnp.sum(total, axis=0, keepdims=True), out)
    else:
        out[...] = total


def side_i(pos, table, row):
    for n in range(16):
        at = pos[2 + n] * 8
        terms = [table[at + k] for k in range(8)]
        while len(terms) > 1:
            terms = [a + b for a, b in zip(terms[::2], terms[1::2])]
        row[:, n * QB : (n + 1) * QB] = terms[0]


def apply_k(v, ks, columns=slice(None)):
    n0 = NI // len(ks)
    terms = [dot(v[:, n * n0 : (n + 1) * n0], k[:, columns], NN) for n, k in enumerate(ks)]
    return (terms[0] + terms[1]) + (terms[2] + terms[3])


def degree_kernel(pos, k0, k1, k2, k3, table, dens_i, out):
    side_i(pos, table, dens_i)
    dens_i[...] = dens_i[...] * (1.0 / NTOT)
    inverse = jnp.broadcast_to(1.0 / dens_i[...], (8, NI)).astype(BF16)
    spread(apply_k(inverse, (k0, k1, k2, k3))[0:1], out)


def half(c):
    return pl.ds(pl.multiple_of(c * CB, CB), CB)


def first_kernel(
    pos, k0, k1, k2, k3, g0, g1, g2, g3, dens_i, table,
    vec, weight_i, weight_log, away, row,
):
    side_i(pos, table, row)
    row[...] = row[...] / (NTOT * dens_i[...])
    weight_i[...] = 1.0 / (dens_i[...] * jnp.sqrt(row[...]))
    weight_log[0:1, :] = weight_i[:, :QB]
    weight_log[1:2, :] = jnp.log(row[:, :QB])
    weight_log[2:, :] = jnp.zeros((6, QB), F32)
    for g, ref in enumerate((g0, g1, g2, g3)):
        for n in range(4):
            at = (4 * g + n) * QB
            for h in range(2):
                both = ref[n, QB + 2 * h * KV : QB + 2 * (h + 1) * KV, :].astype(F32)
                lo = at + h * 128
                part = (both[:KV] + both[KV:]) * weight_i[:, lo : lo + 128]
                vec[:, lo : lo + 128] = part.astype(BF16)
    away[...] = apply_k(vec, (k0, k1, k2, k3), half(1 - pos[1]))


def own_kernel(pos, k0, k1, k2, k3, vec, own):
    y = apply_k(vec, (k0, k1, k2, k3), half(pos[1]))
    if vec.shape[0] == 2 * KV:
        y = y[:KV] + y[KV:]
    own[...] = y


def next_kernel(pos, k0, k1, k2, k3, weight_i, pieces, vec, gram, away, parts):
    for n in range(16):
        at = n * QB
        p = pieces[pos[2 + n]]
        v = p * weight_i[0:1, at : at + QB]
        hi = v.astype(BF16)
        vec[0:KV, at : at + QB] = hi
        vec[KV:, at : at + QB] = (v - hi.astype(F32)).astype(BF16)
        p1 = p.astype(BF16)
        r1 = p - p1.astype(F32)
        p2 = r1.astype(BF16)
        parts[0:KV, at : at + QB] = p1
        parts[KV : 2 * KV, at : at + QB] = p2
        parts[2 * KV :, at : at + QB] = (r1 - p2.astype(F32)).astype(BF16)
    s = dot(parts[...], parts[...], NT)
    rows = s[0:KV] + s[KV : 2 * KV] + s[2 * KV :]
    square = rows[:, 0:KV] + rows[:, KV : 2 * KV] + rows[:, 2 * KV :]
    square = jnp.concatenate([square, jnp.zeros((KV, 128 - KV), F32)], axis=1)
    gram[...] = square
    y2 = apply_k(vec, (k0, k1, k2, k3), half(1 - pos[1]))
    away[:, :CB] = y2[0:KV] + y2[KV:]
    away[:, CB:] = square


def core_sum_kernel(pos, own, away, *refs):
    outs = refs[-4:]
    x = pos[0]
    total = own[...] + away[:, :CB]
    for t in range(4):
        for d in range(4):

            @pl.when((x ^ d) == t)
            def _(t=t, d=d):
                outs[d][:KV, :QB] = total[:, t * QB : (t + 1) * QB]

    if away.shape[1] > CB:
        gram = refs[0][...] + away[:, CB:]
        for ref in outs:
            ref[:, QB:] = gram
    else:
        for ref in outs:
            ref[KV:, :] = refs[0][...]


def core_add_kernel(own, away, gram, out):
    out[:, :CB] = own[...] + away[:, :CB]
    out[:, CB:] = gram[...] + away[:, CB:]


def eliminate(gram, y):
    row = lax.broadcasted_iota(jnp.int32, (KV, 1), 0)
    pivots = jnp.zeros((KV, 1), F32)
    for k in range(KV):
        pivot = gram[k : k + 1, k : k + 1]
        ratio = jnp.where(row > k, gram[:, k : k + 1] * (1.0 / pivot), 0.0)
        pivots = jnp.where(row == k, pivot, pivots)
        gram, y = gram - ratio * gram[k : k + 1, :], y - ratio * y[k : k + 1, :]
    return y * (1.0 / jnp.sqrt(pivots))


def project_first_kernel(pos, weight_log, q0, q1, q2, q3, out, weight_own, log_degree):
    y = (q0[:KV] + q1[:KV]) + (q2[:KV] + q3[:KV])
    p = y * weight_log[0:1, :]
    for n in range(16):
        out[n] = p
    for d, ref in enumerate((q0, q1, q2, q3)):
        at = pl.ds(pl.multiple_of((pos[0] ^ d) * QB, QB), QB)
        weight_own[:, at] = ref[KV : KV + 1, :]
        log_degree[:, at] = ref[KV + 1 : KV + 2, :]


def project_kernel(weight_log, q0, q1, q2, q3, out):
    total = (q0[...] + q1[...]) + (q2[...] + q3[...])
    p = eliminate(total[:, QB:], total[:, :QB]) * weight_log[0:1, :]
    for n in range(16):
        out[n] = p


def last_kernel(weight_own, q0, q1, q2, q3, proj, grams):
    total = (q0[...] + q1[...]) + (q2[...] + q3[...])
    y = eliminate(total[:, CB:], total[:, :CB])
    p = y * weight_own[...]
    proj[...] = p
    gram = lax.dot_general(p, p, NT, precision=lax.Precision.HIGHEST, preferred_element_type=F32)
    gram = jnp.concatenate([gram[:8], gram[8:], jnp.zeros((8, 128 - 2 * KV), F32)], axis=1)
    for n in range(32):
        grams[n] = gram


def finish_kernel(proj, grams, out):
    terms = [grams[n] for n in range(32)]
    while len(terms) > 1:
        terms = [a + b for a, b in zip(terms[::2], terms[1::2])]
    wide = terms[0]
    gram = jnp.concatenate([wide[:, :KV], wide[:, KV : 2 * KV]], axis=0)
    gram = jnp.concatenate([gram, jnp.zeros((KV, 128 - KV), F32)], axis=1)
    lane = lax.broadcasted_iota(jnp.int32, (KV, 128), 1)
    row = lax.broadcasted_iota(jnp.int32, (KV, 128), 0)
    factor = eliminate(gram, jnp.where(lane == row, math.sqrt(NTOT), 0.0))
    p = proj[...]
    terms = [factor[:, k : k + 1] * p[k : k + 1, :] for k in range(KV)]
    while len(terms) > 1:
        terms = [a + b for a, b in zip(terms[::2], terms[1::2])]
    out[...] = terms[0]


def device_number(x, z, y, c):
    return ((x * 4 + z) * 4 + y) * 2 + c


def shift(v, source):
    pairs = [
        (device_number(*source(x, z, y, c)), device_number(x, z, y, c))
        for x in range(4)
        for z in range(4)
        for y in range(4)
        for c in range(2)
    ]
    return lax.ppermute(v, ("x", "z", "y", "c"), pairs)


def from_line(v, d, second=False):
    def source(x, z, y, c):
        along_y = (c == 0) != second
        return (x, z, y ^ d, c) if along_y else (x, z ^ d, y, c)

    return shift(v, source)


def from_x(v, d):
    return shift(v, lambda x, z, y, c: (x ^ d, z, y, c))


def from_core(v):
    return shift(v, lambda x, z, y, c: (x, z, y, 1 - c))


def body(frames, width_class, start):
    x, z, y, c = (lax.axis_index(a) for a in ("x", "z", "y", "c"))
    second, first = jnp.arange(16, dtype=jnp.int32) // 4, jnp.arange(16, dtype=jnp.int32) % 4
    piece_y = y ^ jnp.where(c == 0, first, second)
    piece_z = z ^ jnp.where(c == 0, second, first)
    pos = jnp.concatenate([jnp.stack([x, c]), piece_y * 4 + piece_z]).astype(jnp.int32)

    classes = width_class.reshape(8, 128)
    piece, cls, mine = call(
        pack_kernel,
        "pack",
        [sds((PROWS, F), BF16), sds((16, 128), BF16), vmem((CB, F), BF16)],
        (pos, *(pltpu.with_memory_space_constraint(a, pltpu.HBM) for a in (frames, classes, start))),
        scratch=[
            pltpu.VMEM((KV, QB), F32),
            pltpu.VMEM((8, 128), jnp.int32),
            pltpu.SemaphoreType.DMA((4,)),
        ],
        far=(1, 2, 3),
    )
    line = [piece] + [from_line(piece, d) for d in (1, 2, 3)]
    aug_j, coef_j = call(
        side_kernel,
        "side",
        [sds((NJ, 2 * F), BF16), sds((1, NJ))],
        (pos, keep(mine), cls, from_core(frames), from_core(cls)),
        flops=NJ * 4000,
    )
    line = call(stack_kernel, "stack", sds((4, PROWS, F), BF16), (*line, coef_j))
    groups = [line] + [from_line(line, d, True) for d in (1, 2, 3)]
    ks, sums = [None] * 4, ()
    for g in GROUPS:
        ks[g], sums = call(
            functools.partial(rows_kernel, g),
            f"rows{g}",
            [vmem((4 * QB, NJ), BF16), sds((128, 1, QB) if g == LAST_GROUP else (8, NJ))],
            (pos, groups[g], aug_j, coef_j) + (() if g == 0 else (sums,)),
            flops=4 * QB * NJ * 1024,
        )

    def tile():
        return [keep(k) for k in ks]

    everyone = ("y", "z", "x", "c")
    dens_i, table = call(
        degree_kernel,
        "degree",
        [sds((1, NI)), sds((128, 1, QB))],
        (pos, *tile(), lax.all_to_all(sums, everyone, 0, 0)),
    )
    vec, weight_i, weight_log, away = call(
        first_kernel,
        "first",
        [sds((KV, NI), BF16), sds((1, NI)), sds((8, QB)), sds((KV, CB))],
        (pos, *tile(), *groups, dens_i, lax.all_to_all(table, everyone, 0, 0)),
        scratch=[pltpu.VMEM((1, NI), F32)],
    )
    flops = 2 * NI * CB * 256

    def own_half(iteration):
        return call(own_kernel, f"own{iteration}", sds((KV, CB)), (pos, *tile(), vec), flops=flops)

    for iteration in range(1, ITERS):
        shape = (KV + 8, QB) if iteration == 1 else (KV, QB + 128)
        quarters = call(
            core_sum_kernel,
            f"core_sum{iteration}",
            [sds(shape)] * 4,
            (pos, own_half(iteration), from_core(away), weight_log if iteration == 1 else square),
        )
        quarters = [quarters[0]] + [from_x(quarters[d], d) for d in (1, 2, 3)]
        if iteration == 1:
            pieces, weight_own, log_degree = call(
                project_first_kernel,
                "project1",
                [sds((16, KV, QB)), sds((1, CB)), sds((1, CB))],
                (pos, weight_log, *quarters),
            )
        else:
            pieces = call(
                project_kernel,
                f"project{iteration}",
                sds((16, KV, QB)),
                (weight_log, *quarters),
            )
        pieces = lax.all_to_all(pieces, ("y", "z"), 0, 0)
        vec, square, away = call(
            next_kernel,
            f"next{iteration}",
            [sds((2 * KV, NI), BF16), sds((KV, 128)), sds((KV, CB + 128))],
            (pos, *tile(), weight_i, pieces),
            scratch=[pltpu.VMEM((3 * KV, NI), BF16)],
        )
    total = call(
        core_add_kernel,
        "core_add",
        sds((KV, CB + 128)),
        (own_half(ITERS), from_core(away), square),
    )
    totals = [total] + [from_x(total, d) for d in (1, 2, 3)]
    proj, grams = call(
        last_kernel, "last", [sds((KV, CB)), sds((32, 8, 128))], (weight_own, *totals)
    )
    grams = lax.all_to_all(grams, ("z", "y", "c"), 0, 0)
    embedding = call(finish_kernel, "finish", sds((KV, CB)), (proj, grams))
    return embedding, log_degree.reshape(CB)


def solution(mesh):
    grid = Mesh(mesh.devices.reshape(4, 4, 4, 2), ("x", "z", "y", "c"))
    col = ("z", "y", "c")
    in_specs = (P(col, None), P(col), P(None, col))
    out_specs = (P(None, col), P(col))
    return jax.shard_map(body, mesh=grid, in_specs=in_specs, out_specs=out_specs, check_vma=False)
```

```python
import functools
import math

import jax
import jax.numpy as jnp
from jax import lax
from jax.experimental import pallas as pl
from jax.experimental.pallas import tpu as pltpu
from jax.sharding import Mesh
from jax.sharding import PartitionSpec as P


ITERS = 3
F = 128
CB = 1024
QB = CB // 4
NJ = 2 * CB
NI = 16 * QB
KV = 16
NTOT = 32768
GROUPS = (0, 1, 3, 2)
LAST_GROUP = GROUPS[-1]
CLS = QB + 4 * KV
PROWS = CLS + 16
base_width = 2.8
width_growth = 1.3
F32 = jnp.float32
BF16 = jnp.bfloat16
VM = pltpu.VMEM
NN = (((1,), (0,)), ((), ()))
NT = (((1,), (1,)), ((), ()))
TN = (((0,), (0,)), ((), ()))


def dot(a, b, dims):
    return lax.dot_general(a, b, dims, preferred_element_type=F32)


def call(kernel, name, outs, args, flops=0, scratch=(), far=()):
    def spec(n, a):
        if a.dtype == jnp.int32 and a.ndim == 1:
            return pl.BlockSpec(memory_space=pltpu.SMEM)
        return pl.BlockSpec(memory_space=pltpu.HBM if n in far else VM)

    return pl.pallas_call(
        kernel,
        out_shape=outs,
        in_specs=[spec(n, a) for n, a in enumerate(args)],
        out_specs=jax.tree.map(lambda _: pl.BlockSpec(memory_space=VM), outs),
        scratch_shapes=scratch,
        compiler_params=pltpu.CompilerParams(vmem_limit_bytes=24 << 20),
        cost_estimate=pl.CostEstimate(flops=flops, bytes_accessed=0, transcendentals=0),
        name=name,
    )(*args)


def sds(shape, dtype=F32):
    return jax.ShapeDtypeStruct(shape, dtype)


def vmem(shape, dtype=F32):
    return pltpu.VMEM(shape, dtype)


def keep(a):
    return pltpu.with_memory_space_constraint(a, VM)


def pack_kernel(pos, frames, classes, start, piece, cls_out, mine, quarter, own_classes, sems):
    x = pos[0]
    at = pl.multiple_of(pos[0] * QB, QB)
    copies = (
        pltpu.make_async_copy(frames.at[pl.ds(at, QB), :], piece.at[0:QB, :], sems.at[0]),
        pltpu.make_async_copy(start.at[:, pl.ds(at, QB)], quarter, sems.at[1]),
        pltpu.make_async_copy(classes, own_classes, sems.at[2]),
        pltpu.make_async_copy(frames, mine, sems.at[3]),
    )
    for copy in copies:
        copy.start()
    for copy in copies:
        copy.wait()
    cls_out[...] = own_classes[...]
    wide = piece[0:QB, :].astype(F32)
    square = wide * wide
    upper = square.astype(BF16)
    lower = (square - upper.astype(F32)).astype(BF16)
    ones = jnp.ones((8, F), BF16)
    half = -0.5 * (dot(ones, upper, NT) + dot(ones, lower, NT))[0:1]
    p1 = half.astype(BF16).astype(F32)
    p2 = (half - p1).astype(BF16).astype(F32)
    extra = [p[:, h * 128 : (h + 1) * 128] for p in (p1, p2, half - p1 - p2) for h in range(2)]
    extra.append(own_classes[pl.ds(2 * x, 1), :].astype(F32))
    extra.append(own_classes[pl.ds(2 * x + 1, 1), :].astype(F32))
    extra.append(jnp.ones((8, 128), F32))
    piece[CLS:PROWS, :] = jnp.concatenate(extra, axis=0).astype(BF16)
    high = quarter[...].astype(BF16)
    low = (quarter[...] - high.astype(F32)).astype(BF16)
    for h in range(2):
        at = QB + 2 * h * KV
        piece[at : at + KV, :] = high[:, h * 128 : (h + 1) * 128]
        piece[at + KV : at + 2 * KV, :] = low[:, h * 128 : (h + 1) * 128]


def stack_kernel(a, b, d, c, ready, out):
    del ready
    for n, ref in enumerate((a, b, c, d)):
        out[n] = ref[...]


def augment(rows):
    wide = rows.astype(F32)
    half = -0.5 * jnp.sum(wide * wide, axis=1, keepdims=True)
    p1 = half.astype(BF16).astype(F32)
    p2 = (half - p1).astype(BF16).astype(F32)
    lane = lax.broadcasted_iota(jnp.int32, (rows.shape[0], 128), 1)
    extra = jnp.where(lane < 3, 1.0, 0.0)
    for n, part in enumerate((p1, p2, half - p1 - p2)):
        extra = jnp.where(lane == 3 + n, part, extra)
    return jnp.concatenate([rows, extra.astype(BF16)], axis=1)


def inverse_width(cls):
    return jnp.exp2(cls * (-math.log2(width_growth))) * (1.0 / base_width)


def side_kernel(rows, cls, aug_j, coef_j):
    aug_j[...] = augment(rows[...])
    coef = inverse_width(cls[...].astype(F32)) * (2.0 * math.log2(math.e))
    for r in range(8):
        coef_j[:, r * 128 : (r + 1) * 128] = coef[r : r + 1, :]


def spread(row, c, out):
    for quarter in range(4):
        lo = quarter * QB
        own, other = row[:, lo : lo + QB], row[:, CB + lo : CB + lo + QB]
        for core in range(2):
            value = jnp.where(c == core, own, other)
            for n in range(16):
                out[8 * n + 2 * quarter + core] = value


def rows_kernel(group, pos, pieces, aug_own, coef_own, aug_other, coef_other, *refs):
    k_ref, out = refs[-2:]
    row = lax.broadcasted_iota(jnp.int32, (16, 128), 0)
    lane = lax.broadcasted_iota(jnp.int32, (16, 128), 1)
    picks = []
    for h in range(2):
        parts = jnp.logical_and(lane < 3, row == 2 * lane + h)
        ones = jnp.logical_and(jnp.logical_and(lane >= 3, lane < 6), row == 8)
        cls = jnp.logical_and(lane == 8, row == 6 + h)
        pick = jnp.logical_or(jnp.logical_or(parts, ones), cls)
        picks.append(jnp.where(pick, 1.0, 0.0).astype(BF16))
    half = 512
    sides = ((0, aug_own, coef_own), (CB, aug_other, coef_other))
    totals = [jnp.zeros((8, CB), F32) if group == 0 else refs[0][:, lo : lo + CB] for lo, _, _ in sides]
    for n in range(2):
        columns = [
            dot(pieces[m, CLS:PROWS, :], pick, TN) for m in (2 * n, 2 * n + 1) for pick in picks
        ]
        columns = jnp.concatenate(columns, axis=0)
        rows = jnp.concatenate([pieces[2 * n, 0:QB, :], pieces[2 * n + 1, 0:QB, :]], axis=0)
        aug_i = jnp.concatenate([rows, columns.astype(BF16)], axis=1)
        coef_i = inverse_width(columns[:, 8:9])
        for s, (lo, aug, coef) in enumerate(sides):
            e = jnp.exp2(dot(aug_i, aug[...], NT) * coef_i * coef[...])
            k_ref[n * half : (n + 1) * half, lo : lo + CB] = e.astype(BF16)
            totals[s] = totals[s] + jnp.sum(e.reshape(half // 8, 8, CB), axis=0)
    if group == LAST_GROUP:
        total = jnp.concatenate(totals, axis=1)
        spread(jnp.sum(total, axis=0, keepdims=True), pos[1], out)
    else:
        for total, (lo, _, _) in zip(totals, sides):
            out[:, lo : lo + CB] = total


def side_i(pos, table, row):
    for n in range(16):
        at = pos[2 + n] * 8
        terms = [table[at + k] for k in range(8)]
        while len(terms) > 1:
            terms = [a + b for a, b in zip(terms[::2], terms[1::2])]
        row[:, n * QB : (n + 1) * QB] = terms[0]


def apply_k(v, ks, columns=slice(None)):
    n0 = NI // len(ks)
    terms = [dot(v[:, n * n0 : (n + 1) * n0], k[:, columns], NN) for n, k in enumerate(ks)]
    return (terms[0] + terms[1]) + (terms[2] + terms[3])


def degree_kernel(pos, k0, k1, k2, k3, table, dens_i, out):
    side_i(pos, table, dens_i)
    dens_i[...] = dens_i[...] * (1.0 / NTOT)
    inverse = jnp.broadcast_to(1.0 / dens_i[...], (8, NI)).astype(BF16)
    spread(apply_k(inverse, (k0, k1, k2, k3))[0:1], pos[1], out)


OWN, AWAY = slice(0, CB), slice(CB, NJ)


def first_kernel(
    pos, k0, k1, k2, k3, g0, g1, g2, g3, dens_i, table,
    vec, weight_i, weight_log, away, row,
):
    side_i(pos, table, row)
    row[...] = row[...] / (NTOT * dens_i[...])
    weight_i[...] = 1.0 / (dens_i[...] * jnp.sqrt(row[...]))
    weight_log[0:1, :] = weight_i[:, :QB]
    weight_log[1:2, :] = jnp.log(row[:, :QB])
    weight_log[2:, :] = jnp.zeros((6, QB), F32)
    for g, ref in enumerate((g0, g1, g2, g3)):
        for n in range(4):
            at = (4 * g + n) * QB
            for h in range(2):
                both = ref[n, QB + 2 * h * KV : QB + 2 * (h + 1) * KV, :].astype(F32)
                lo = at + h * 128
                part = (both[:KV] + both[KV:]) * weight_i[:, lo : lo + 128]
                vec[:, lo : lo + 128] = part.astype(BF16)
    away[...] = apply_k(vec, (k0, k1, k2, k3), AWAY)


def own_kernel(k0, k1, k2, k3, vec, own):
    y = apply_k(vec, (k0, k1, k2, k3), OWN)
    if vec.shape[0] == 2 * KV:
        y = y[:KV] + y[KV:]
    own[...] = y


def next_kernel(pos, k0, k1, k2, k3, weight_i, pieces, vec, gram, away, parts):
    for n in range(16):
        at = n * QB
        p = pieces[pos[2 + n]]
        v = p * weight_i[0:1, at : at + QB]
        hi = v.astype(BF16)
        vec[0:KV, at : at + QB] = hi
        vec[KV:, at : at + QB] = (v - hi.astype(F32)).astype(BF16)
        p1 = p.astype(BF16)
        r1 = p - p1.astype(F32)
        p2 = r1.astype(BF16)
        parts[0:KV, at : at + QB] = p1
        parts[KV : 2 * KV, at : at + QB] = p2
        parts[2 * KV :, at : at + QB] = (r1 - p2.astype(F32)).astype(BF16)
    s = dot(parts[...], parts[...], NT)
    rows = s[0:KV] + s[KV : 2 * KV] + s[2 * KV :]
    square = rows[:, 0:KV] + rows[:, KV : 2 * KV] + rows[:, 2 * KV :]
    square = jnp.concatenate([square, jnp.zeros((KV, 128 - KV), F32)], axis=1)
    gram[...] = square
    y2 = apply_k(vec, (k0, k1, k2, k3), AWAY)
    away[:, :CB] = y2[0:KV] + y2[KV:]
    away[:, CB:] = square


def core_sum_kernel(pos, own, away, *refs):
    outs = refs[-4:]
    x = pos[0]
    total = own[...] + away[:, :CB]
    for t in range(4):
        for d in range(4):

            @pl.when((x ^ d) == t)
            def _(t=t, d=d):
                outs[d][:KV, :QB] = total[:, t * QB : (t + 1) * QB]

    if away.shape[1] > CB:
        gram = refs[0][...] + away[:, CB:]
        for ref in outs:
            ref[:, QB:] = gram
    else:
        for ref in outs:
            ref[KV:, :] = refs[0][...]


def core_add_kernel(own, away, gram, out):
    out[:, :CB] = own[...] + away[:, :CB]
    out[:, CB:] = gram[...] + away[:, CB:]


def eliminate(gram, y):
    row = lax.broadcasted_iota(jnp.int32, (KV, 1), 0)
    pivots = jnp.zeros((KV, 1), F32)
    for k in range(KV):
        pivot = gram[k : k + 1, k : k + 1]
        ratio = jnp.where(row > k, gram[:, k : k + 1] * (1.0 / pivot), 0.0)
        pivots = jnp.where(row == k, pivot, pivots)
        gram, y = gram - ratio * gram[k : k + 1, :], y - ratio * y[k : k + 1, :]
    return y * (1.0 / jnp.sqrt(pivots))


def project_first_kernel(pos, weight_log, q0, q1, q2, q3, out, weight_own, log_degree):
    y = (q0[:KV] + q1[:KV]) + (q2[:KV] + q3[:KV])
    p = y * weight_log[0:1, :]
    for n in range(16):
        out[n] = p
    for d, ref in zip((0, 2, 1, 3), (q0, q1, q2, q3)):
        at = pl.ds(pl.multiple_of((pos[0] ^ d) * QB, QB), QB)
        weight_own[:, at] = ref[KV : KV + 1, :]
        log_degree[:, at] = ref[KV + 1 : KV + 2, :]


def project_kernel(weight_log, q0, q1, q2, q3, out):
    total = (q0[...] + q1[...]) + (q2[...] + q3[...])
    p = eliminate(total[:, QB:], total[:, :QB]) * weight_log[0:1, :]
    for n in range(16):
        out[n] = p


def last_kernel(weight_own, q0, q1, q2, q3, proj, grams):
    total = (q0[...] + q1[...]) + (q2[...] + q3[...])
    y = eliminate(total[:, CB:], total[:, :CB])
    p = y * weight_own[...]
    proj[...] = p
    gram = lax.dot_general(p, p, NT, precision=lax.Precision.HIGHEST, preferred_element_type=F32)
    gram = jnp.concatenate([gram[:8], gram[8:], jnp.zeros((8, 128 - 2 * KV), F32)], axis=1)
    for n in range(32):
        grams[n] = gram


def finish_kernel(proj, grams, out):
    terms = [grams[n] for n in range(32)]
    while len(terms) > 1:
        terms = [a + b for a, b in zip(terms[::2], terms[1::2])]
    wide = terms[0]
    gram = jnp.concatenate([wide[:, :KV], wide[:, KV : 2 * KV]], axis=0)
    gram = jnp.concatenate([gram, jnp.zeros((KV, 128 - KV), F32)], axis=1)
    lane = lax.broadcasted_iota(jnp.int32, (KV, 128), 1)
    row = lax.broadcasted_iota(jnp.int32, (KV, 128), 0)
    factor = eliminate(gram, jnp.where(lane == row, math.sqrt(NTOT), 0.0))
    p = proj[...]
    terms = [factor[:, k : k + 1] * p[k : k + 1, :] for k in range(KV)]
    while len(terms) > 1:
        terms = [a + b for a, b in zip(terms[::2], terms[1::2])]
    out[...] = terms[0]


def device_number(x, z, y, c):
    return ((x * 4 + z) * 4 + y) * 2 + c


def shift(v, source):
    pairs = [
        (device_number(*source(x, z, y, c)), device_number(x, z, y, c))
        for x in range(4)
        for z in range(4)
        for y in range(4)
        for c in range(2)
    ]
    return lax.ppermute(v, ("x", "z", "y", "c"), pairs)


def from_line(v, d, second=False):
    def source(x, z, y, c):
        along_y = (c == 0) != second
        return (x, z, y ^ d, c) if along_y else (x, z ^ d, y, c)

    return shift(v, source)


def from_x(v, d):
    return shift(v, lambda x, z, y, c: (x ^ d, z, y, c))


def from_core(v):
    return shift(v, lambda x, z, y, c: (x, z, y, 1 - c))


def body(frames, width_class, start):
    x, z, y, c = (lax.axis_index(a) for a in ("x", "z", "y", "c"))
    second, first = jnp.arange(16, dtype=jnp.int32) // 4, jnp.arange(16, dtype=jnp.int32) % 4
    piece_y = y ^ jnp.where(c == 0, first, second)
    piece_z = z ^ jnp.where(c == 0, second, first)
    pos = jnp.concatenate([jnp.stack([x, c]), piece_y * 4 + piece_z]).astype(jnp.int32)

    classes = width_class.reshape(8, 128)
    piece, cls, mine = call(
        pack_kernel,
        "pack",
        [sds((PROWS, F), BF16), sds((8, 128), jnp.int32), vmem((CB, F), BF16)],
        (pos, *(pltpu.with_memory_space_constraint(a, pltpu.HBM) for a in (frames, classes, start))),
        scratch=[
            pltpu.VMEM((KV, QB), F32),
            pltpu.VMEM((8, 128), jnp.int32),
            pltpu.SemaphoreType.DMA((4,)),
        ],
        far=(1, 2, 3),
    )
    line = [piece] + [from_line(piece, d) for d in (1, 3, 2)]
    shapes = [sds((CB, 2 * F), BF16), sds((1, CB))]
    own_side = call(side_kernel, "own_side", shapes, (keep(mine), cls), flops=CB * 4000)
    sides = own_side + call(
        side_kernel, "other_side", shapes, (from_core(frames), from_core(classes)), flops=CB * 4000
    )
    line = call(
        stack_kernel, "stack", sds((4, PROWS, F), BF16), (*line, own_side[1])
    )
    groups = [line] + [from_line(line, d, True) for d in (1, 2, 3)]
    ks, sums = [None] * 4, ()
    for g in GROUPS:
        ks[g], sums = call(
            functools.partial(rows_kernel, g),
            f"rows{g}",
            [vmem((4 * QB, NJ), BF16), sds((128, 1, QB) if g == LAST_GROUP else (8, NJ))],
            (pos, groups[g], *sides) + (() if g == 0 else (sums,)),
            flops=4 * QB * NJ * 1024,
        )

    def tile():
        return [keep(k) for k in ks]

    everyone = ("y", "z", "x", "c")
    dens_i, table = call(
        degree_kernel,
        "degree",
        [sds((1, NI)), sds((128, 1, QB))],
        (pos, *tile(), lax.all_to_all(sums, everyone, 0, 0)),
    )
    vec, weight_i, weight_log, away = call(
        first_kernel,
        "first",
        [sds((KV, NI), BF16), sds((1, NI)), sds((8, QB)), sds((KV, CB))],
        (pos, *tile(), *groups, dens_i, lax.all_to_all(table, everyone, 0, 0)),
        scratch=[pltpu.VMEM((1, NI), F32)],
    )
    flops = 2 * NI * CB * 256

    def own_half(iteration):
        return call(own_kernel, f"own{iteration}", sds((KV, CB)), (*tile(), vec), flops=flops)

    for iteration in range(1, ITERS):
        shape = (KV + 8, QB) if iteration == 1 else (KV, QB + 128)
        quarters = call(
            core_sum_kernel,
            f"core_sum{iteration}",
            [sds(shape)] * 4,
            (pos, own_half(iteration), from_core(away), weight_log if iteration == 1 else square),
        )
        quarters = [quarters[0]] + [from_x(quarters[d], d) for d in (2, 1, 3)]
        if iteration == 1:
            pieces, weight_own, log_degree = call(
                project_first_kernel,
                "project1",
                [sds((16, KV, QB)), sds((1, CB)), sds((1, CB))],
                (pos, weight_log, *quarters),
            )
        else:
            pieces = call(
                project_kernel,
                f"project{iteration}",
                sds((16, KV, QB)),
                (weight_log, *quarters),
            )
        pieces = lax.all_to_all(pieces, ("y", "z"), 0, 0)
        vec, square, away = call(
            next_kernel,
            f"next{iteration}",
            [sds((2 * KV, NI), BF16), sds((KV, 128)), sds((KV, CB + 128))],
            (pos, *tile(), weight_i, pieces),
            scratch=[pltpu.VMEM((3 * KV, NI), BF16)],
        )
    total = call(
        core_add_kernel,
        "core_add",
        sds((KV, CB + 128)),
        (own_half(ITERS), from_core(away), square),
    )
    totals = [total] + [from_x(total, d) for d in (1, 3, 2)]
    proj, grams = call(
        last_kernel, "last", [sds((KV, CB)), sds((32, 8, 128))], (weight_own, *totals)
    )
    grams = lax.all_to_all(grams, ("z", "y", "c"), 0, 0)
    embedding = call(finish_kernel, "finish", sds((KV, CB)), (proj, grams))
    return embedding, log_degree.reshape(CB)


def solution(mesh):
    grid = Mesh(mesh.devices.reshape(4, 4, 4, 2), ("x", "z", "y", "c"))
    col = ("z", "y", "c")
    in_specs = (P(col, None), P(col), P(None, col))
    out_specs = (P(None, col), P(col))
    return jax.shard_map(body, mesh=grid, in_specs=in_specs, out_specs=out_specs, check_vma=False)
```

```python
import functools
import math

import jax
import jax.numpy as jnp
from jax import lax
from jax.experimental import pallas as pl
from jax.experimental.pallas import tpu as pltpu
from jax.sharding import Mesh
from jax.sharding import PartitionSpec as P


ITERS = 3
F = 128
CB = 1024
QB = CB // 4
NJ = 2 * CB
NI = 16 * QB
KV = 16
NTOT = 32768
CLS = QB + 4 * KV
PROWS = CLS + 16
base_width = 2.8
width_growth = 1.3
F32 = jnp.float32
BF16 = jnp.bfloat16
VM = pltpu.VMEM
NN = (((1,), (0,)), ((), ()))
NT = (((1,), (1,)), ((), ()))
TN = (((0,), (0,)), ((), ()))


def dot(a, b, dims):
    return lax.dot_general(a, b, dims, preferred_element_type=F32)


def call(kernel, name, outs, args, flops=0, scratch=(), far=()):
    def spec(n, a):
        if a.dtype == jnp.int32 and a.ndim == 1:
            return pl.BlockSpec(memory_space=pltpu.SMEM)
        return pl.BlockSpec(memory_space=pltpu.HBM if n in far else VM)

    return pl.pallas_call(
        kernel,
        out_shape=outs,
        in_specs=[spec(n, a) for n, a in enumerate(args)],
        out_specs=jax.tree.map(lambda _: pl.BlockSpec(memory_space=VM), outs),
        scratch_shapes=scratch,
        compiler_params=pltpu.CompilerParams(vmem_limit_bytes=24 << 20),
        cost_estimate=pl.CostEstimate(flops=flops, bytes_accessed=0, transcendentals=0),
        name=name,
    )(*args)


def sds(shape, dtype=F32):
    return jax.ShapeDtypeStruct(shape, dtype)


def vmem(shape, dtype=F32):
    return pltpu.VMEM(shape, dtype)


def keep(a):
    return pltpu.with_memory_space_constraint(a, VM)


def pack_kernel(pos, frames, classes, start, piece, mine, quarter, own_classes, sems):
    x = pos[0]
    at = pl.multiple_of(pos[0] * QB, QB)
    copies = (
        pltpu.make_async_copy(frames.at[pl.ds(at, QB), :], piece.at[0:QB, :], sems.at[0]),
        pltpu.make_async_copy(start.at[:, pl.ds(at, QB)], quarter, sems.at[1]),
        pltpu.make_async_copy(classes, own_classes, sems.at[2]),
        pltpu.make_async_copy(frames, mine.at[0:CB, :], sems.at[3]),
    )
    for copy in copies:
        copy.start()
    for copy in copies:
        copy.wait()
    cls = own_classes[...].astype(F32)
    mine[CB:, :] = jnp.concatenate([cls, jnp.zeros_like(cls)], axis=0).astype(BF16)
    wide = piece[0:QB, :].astype(F32)
    square = wide * wide
    upper = square.astype(BF16)
    lower = (square - upper.astype(F32)).astype(BF16)
    ones = jnp.ones((8, F), BF16)
    half = -0.5 * (dot(ones, upper, NT) + dot(ones, lower, NT))[0:1]
    p1 = half.astype(BF16).astype(F32)
    p2 = (half - p1).astype(BF16).astype(F32)
    extra = [p[:, h * 128 : (h + 1) * 128] for p in (p1, p2, half - p1 - p2) for h in range(2)]
    extra.append(own_classes[pl.ds(2 * x, 1), :].astype(F32))
    extra.append(own_classes[pl.ds(2 * x + 1, 1), :].astype(F32))
    extra.append(jnp.ones((8, 128), F32))
    piece[CLS:PROWS, :] = jnp.concatenate(extra, axis=0).astype(BF16)
    high = quarter[...].astype(BF16)
    low = (quarter[...] - high.astype(F32)).astype(BF16)
    for h in range(2):
        at = QB + 2 * h * KV
        piece[at : at + KV, :] = high[:, h * 128 : (h + 1) * 128]
        piece[at + KV : at + 2 * KV, :] = low[:, h * 128 : (h + 1) * 128]


def stack_kernel(a, b, d, c, ready, out):
    del ready
    for n, ref in enumerate((a, b, c, d)):
        out[n] = ref[...]


def augment(rows):
    wide = rows.astype(F32)
    half = -0.5 * jnp.sum(wide * wide, axis=1, keepdims=True)
    p1 = half.astype(BF16).astype(F32)
    p2 = (half - p1).astype(BF16).astype(F32)
    lane = lax.broadcasted_iota(jnp.int32, (rows.shape[0], 128), 1)
    extra = jnp.where(lane < 3, 1.0, 0.0)
    for n, part in enumerate((p1, p2, half - p1 - p2)):
        extra = jnp.where(lane == 3 + n, part, extra)
    return jnp.concatenate([rows, extra.astype(BF16)], axis=1)


def inverse_width(cls):
    return jnp.exp2(cls * (-math.log2(width_growth))) * (1.0 / base_width)


def side_kernel(block, aug_j, coef_j):
    aug_j[...] = augment(block[0:CB, :])
    coef = inverse_width(block[CB:, :].astype(F32)) * (2.0 * math.log2(math.e))
    for r in range(8):
        coef_j[:, r * 128 : (r + 1) * 128] = coef[r : r + 1, :]


def spread(row, c, out):
    for quarter in range(4):
        lo = quarter * QB
        own, other = row[:, lo : lo + QB], row[:, CB + lo : CB + lo + QB]
        for core in range(2):
            value = jnp.where(c == core, own, other)
            for n in range(16):
                out[8 * n + 2 * quarter + core] = value


def rows_kernel(count, first, last, pos, *refs):
    groups, (aug_own, coef_own, aug_other, coef_other) = refs[:count], refs[count : count + 4]
    k_refs, out = refs[-1 - count : -1], refs[-1]
    row = lax.broadcasted_iota(jnp.int32, (16, 128), 0)
    lane = lax.broadcasted_iota(jnp.int32, (16, 128), 1)
    picks = []
    for h in range(2):
        parts = jnp.logical_and(lane < 3, row == 2 * lane + h)
        ones = jnp.logical_and(jnp.logical_and(lane >= 3, lane < 6), row == 8)
        cls = jnp.logical_and(lane == 8, row == 6 + h)
        pick = jnp.logical_or(jnp.logical_or(parts, ones), cls)
        picks.append(jnp.where(pick, 1.0, 0.0).astype(BF16))
    half = 512
    sides = ((0, aug_own, coef_own), (CB, aug_other, coef_other))
    totals = [
        jnp.zeros((8, CB), F32) if first else refs[count + 4][:, lo : lo + CB] for lo, _, _ in sides
    ]
    for pieces, k_ref in zip(groups, k_refs):
        for n in range(2):
            columns = [
                dot(pieces[m, CLS:PROWS, :], pick, TN) for m in (2 * n, 2 * n + 1) for pick in picks
            ]
            columns = jnp.concatenate(columns, axis=0)
            rows = jnp.concatenate([pieces[2 * n, 0:QB, :], pieces[2 * n + 1, 0:QB, :]], axis=0)
            aug_i = jnp.concatenate([rows, columns.astype(BF16)], axis=1)
            coef_i = inverse_width(columns[:, 8:9])
            for s, (lo, aug, coef) in enumerate(sides):
                e = jnp.exp2(dot(aug_i, aug[...], NT) * coef_i * coef[...])
                k_ref[n * half : (n + 1) * half, lo : lo + CB] = e.astype(BF16)
                totals[s] = totals[s] + jnp.sum(e.reshape(half // 8, 8, CB), axis=0)
    if last:
        total = jnp.concatenate(totals, axis=1)
        spread(jnp.sum(total, axis=0, keepdims=True), pos[1], out)
    else:
        for total, (lo, _, _) in zip(totals, sides):
            out[:, lo : lo + CB] = total


def side_i(pos, table, row):
    for n in range(16):
        at = pos[2 + n] * 8
        terms = [table[at + k] for k in range(8)]
        while len(terms) > 1:
            terms = [a + b for a, b in zip(terms[::2], terms[1::2])]
        row[:, n * QB : (n + 1) * QB] = terms[0]


def apply_k(v, ks, columns=slice(None)):
    n0 = NI // len(ks)
    terms = [dot(v[:, n * n0 : (n + 1) * n0], k[:, columns], NN) for n, k in enumerate(ks)]
    return (terms[0] + terms[1]) + (terms[2] + terms[3])


def degree_kernel(pos, k0, k1, k2, k3, table, dens_i, out):
    side_i(pos, table, dens_i)
    dens_i[...] = dens_i[...] * (1.0 / NTOT)
    inverse = jnp.broadcast_to(1.0 / dens_i[...], (8, NI)).astype(BF16)
    spread(apply_k(inverse, (k0, k1, k2, k3))[0:1], pos[1], out)


OWN, AWAY = slice(0, CB), slice(CB, NJ)


def first_kernel(
    pos, k0, k1, k2, k3, g0, g1, g2, g3, dens_i, table,
    vec, weight_i, weight_log, away, row,
):
    side_i(pos, table, row)
    row[...] = row[...] / (NTOT * dens_i[...])
    weight_i[...] = 1.0 / (dens_i[...] * jnp.sqrt(row[...]))
    weight_log[0:1, :] = weight_i[:, :QB]
    weight_log[1:2, :] = jnp.log(row[:, :QB])
    weight_log[2:, :] = jnp.zeros((6, QB), F32)
    for g, ref in enumerate((g0, g1, g2, g3)):
        for n in range(4):
            at = (4 * g + n) * QB
            for h in range(2):
                both = ref[n, QB + 2 * h * KV : QB + 2 * (h + 1) * KV, :].astype(F32)
                lo = at + h * 128
                part = (both[:KV] + both[KV:]) * weight_i[:, lo : lo + 128]
                vec[:, lo : lo + 128] = part.astype(BF16)
    away[...] = apply_k(vec, (k0, k1, k2, k3), AWAY)


def own_kernel(k0, k1, k2, k3, vec, own):
    y = apply_k(vec, (k0, k1, k2, k3), OWN)
    if vec.shape[0] == 2 * KV:
        y = y[:KV] + y[KV:]
    own[...] = y


def next_kernel(pos, k0, k1, k2, k3, weight_i, pieces, vec, gram, away, parts):
    for n in range(16):
        at = n * QB
        p = pieces[pos[2 + n]]
        v = p * weight_i[0:1, at : at + QB]
        hi = v.astype(BF16)
        vec[0:KV, at : at + QB] = hi
        vec[KV:, at : at + QB] = (v - hi.astype(F32)).astype(BF16)
        p1 = p.astype(BF16)
        r1 = p - p1.astype(F32)
        p2 = r1.astype(BF16)
        parts[0:KV, at : at + QB] = p1
        parts[KV : 2 * KV, at : at + QB] = p2
        parts[2 * KV :, at : at + QB] = (r1 - p2.astype(F32)).astype(BF16)
    s = dot(parts[...], parts[...], NT)
    rows = s[0:KV] + s[KV : 2 * KV] + s[2 * KV :]
    square = rows[:, 0:KV] + rows[:, KV : 2 * KV] + rows[:, 2 * KV :]
    square = jnp.concatenate([square, jnp.zeros((KV, 128 - KV), F32)], axis=1)
    gram[...] = square
    y2 = apply_k(vec, (k0, k1, k2, k3), AWAY)
    away[:, :CB] = y2[0:KV] + y2[KV:]
    away[:, CB:] = square


def core_sum_kernel(pos, own, away, *refs):
    outs = refs[-4:]
    for d, out in enumerate(outs):
        at = pl.ds(pl.multiple_of((pos[0] ^ d) * QB, QB), QB)
        out[:KV, :QB] = own[:, at] + away[:, at]
    if away.shape[1] > CB:
        gram = refs[0][...] + away[:, CB:]
        for ref in outs:
            ref[:, QB:] = gram
    else:
        for ref in outs:
            ref[KV:, :] = refs[0][...]


def core_add_kernel(own, away, gram, out):
    out[:, :CB] = own[...] + away[:, :CB]
    out[:, CB:] = gram[...] + away[:, CB:]


def eliminate(gram, y):
    row = lax.broadcasted_iota(jnp.int32, (KV, 1), 0)
    pivots = jnp.zeros((KV, 1), F32)
    for k in range(KV):
        pivot = gram[k : k + 1, k : k + 1]
        ratio = jnp.where(row > k, gram[:, k : k + 1] * (1.0 / pivot), 0.0)
        pivots = jnp.where(row == k, pivot, pivots)
        gram, y = gram - ratio * gram[k : k + 1, :], y - ratio * y[k : k + 1, :]
    return y * (1.0 / jnp.sqrt(pivots))


def project_first_kernel(pos, weight_log, q0, q1, q2, q3, out, weight_own, log_degree):
    y = (q0[:KV] + q1[:KV]) + (q2[:KV] + q3[:KV])
    p = y * weight_log[0:1, :]
    for n in range(16):
        out[n] = p
    for d, ref in zip((0, 2, 1, 3), (q0, q1, q2, q3)):
        at = pl.ds(pl.multiple_of((pos[0] ^ d) * QB, QB), QB)
        weight_own[:, at] = ref[KV : KV + 1, :]
        log_degree[:, at] = ref[KV + 1 : KV + 2, :]


def project_kernel(weight_log, q0, q1, q2, q3, out):
    total = (q0[...] + q1[...]) + (q2[...] + q3[...])
    p = eliminate(total[:, QB:], total[:, :QB]) * weight_log[0:1, :]
    for n in range(16):
        out[n] = p


def last_kernel(weight_own, q0, q1, q2, q3, proj, grams):
    total = (q0[...] + q1[...]) + (q2[...] + q3[...])
    y = eliminate(total[:, CB:], total[:, :CB])
    p = y * weight_own[...]
    proj[...] = p
    gram = lax.dot_general(p, p, NT, precision=lax.Precision.HIGHEST, preferred_element_type=F32)
    gram = jnp.concatenate([gram[:8], gram[8:], jnp.zeros((8, 128 - 2 * KV), F32)], axis=1)
    for n in range(32):
        grams[n] = gram


def finish_kernel(proj, grams, log_in, out, log_degree):
    log_degree[...] = log_in[...]
    terms = [grams[n] for n in range(32)]
    while len(terms) > 1:
        terms = [a + b for a, b in zip(terms[::2], terms[1::2])]
    wide = terms[0]
    gram = jnp.concatenate([wide[:, :KV], wide[:, KV : 2 * KV]], axis=0)
    gram = jnp.concatenate([gram, jnp.zeros((KV, 128 - KV), F32)], axis=1)
    lane = lax.broadcasted_iota(jnp.int32, (KV, 128), 1)
    row = lax.broadcasted_iota(jnp.int32, (KV, 128), 0)
    factor = eliminate(gram, jnp.where(lane == row, math.sqrt(NTOT), 0.0))
    p = proj[...]
    terms = [factor[:, k : k + 1] * p[k : k + 1, :] for k in range(KV)]
    while len(terms) > 1:
        terms = [a + b for a, b in zip(terms[::2], terms[1::2])]
    out[...] = terms[0]


def device_number(x, z, y, c):
    return ((x * 4 + z) * 4 + y) * 2 + c


def shift(v, source):
    pairs = [
        (device_number(*source(x, z, y, c)), device_number(x, z, y, c))
        for x in range(4)
        for z in range(4)
        for y in range(4)
        for c in range(2)
    ]
    return lax.ppermute(v, ("x", "z", "y", "c"), pairs)


def from_line(v, d, second=False):
    def source(x, z, y, c):
        along_y = (c == 0) != second
        return (x, z, y ^ d, c) if along_y else (x, z ^ d, y, c)

    return shift(v, source)


def from_x(v, d):
    return shift(v, lambda x, z, y, c: (x ^ d, z, y, c))


def from_core(v):
    return shift(v, lambda x, z, y, c: (x, z, y, 1 - c))


def body(frames, width_class, start):
    x, z, y, c = (lax.axis_index(a) for a in ("x", "z", "y", "c"))
    second, first = jnp.arange(16, dtype=jnp.int32) // 4, jnp.arange(16, dtype=jnp.int32) % 4
    piece_y = y ^ jnp.where(c == 0, first, second)
    piece_z = z ^ jnp.where(c == 0, second, first)
    pos = jnp.concatenate([jnp.stack([x, c]), piece_y * 4 + piece_z]).astype(jnp.int32)

    classes = width_class.reshape(8, 128)
    piece, mine = call(
        pack_kernel,
        "pack",
        [sds((PROWS, F), BF16), vmem((CB + 16, F), BF16)],
        (pos, *(pltpu.with_memory_space_constraint(a, pltpu.HBM) for a in (frames, classes, start))),
        scratch=[
            pltpu.VMEM((KV, QB), F32),
            pltpu.VMEM((8, 128), jnp.int32),
            pltpu.SemaphoreType.DMA((4,)),
        ],
        far=(1, 2, 3),
    )
    line = [piece] + [from_line(piece, d) for d in (1, 3, 2)]
    shapes = [sds((CB, 2 * F), BF16), sds((1, CB))]
    own_side = call(side_kernel, "own_side", shapes, (keep(mine),), flops=CB * 4000)
    sides = own_side + call(
        side_kernel, "other_side", shapes, (from_core(keep(mine)),), flops=CB * 4000
    )
    line = call(
        stack_kernel, "stack", sds((4, PROWS, F), BF16), (*line, own_side[1])
    )
    groups = [line] + [from_line(line, d, True) for d in (1, 2, 3)]
    ks, sums = [None] * 4, ()
    for step in ((0,), (1,), (2,), (3,)):
        last = step == (3,)
        *made, total = call(
            functools.partial(rows_kernel, len(step), step == (0,), last),
            f"rows{step[0]}",
            [vmem((4 * QB, NJ), BF16)] * len(step) + [sds((128, 1, QB) if last else (8, NJ))],
            (pos, *(groups[g] for g in step), *sides, *sums),
            flops=len(step) * 4 * QB * NJ * 1024,
        )
        sums = (total,)
        for g, k in zip(step, made):
            ks[g] = k

    def tile():
        return [keep(k) for k in ks]

    everyone = ("y", "z", "x", "c")
    dens_i, table = call(
        degree_kernel,
        "degree",
        [sds((1, NI)), sds((128, 1, QB))],
        (pos, *tile(), lax.all_to_all(sums[0], everyone, 0, 0)),
    )
    vec, weight_i, weight_log, away = call(
        first_kernel,
        "first",
        [sds((KV, NI), BF16), sds((1, NI)), sds((8, QB)), sds((KV, CB))],
        (pos, *tile(), *groups, dens_i, lax.all_to_all(table, everyone, 0, 0)),
        scratch=[pltpu.VMEM((1, NI), F32)],
    )
    flops = 2 * NI * CB * 256

    def own_half(iteration):
        return call(own_kernel, f"own{iteration}", sds((KV, CB)), (*tile(), vec), flops=flops)

    for iteration in range(1, ITERS):
        shape = (KV + 8, QB) if iteration == 1 else (KV, QB + 128)
        quarters = call(
            core_sum_kernel,
            f"core_sum{iteration}",
            [sds(shape)] * 4,
            (pos, own_half(iteration), from_core(away), weight_log if iteration == 1 else square),
        )
        quarters = [quarters[0]] + [from_x(quarters[d], d) for d in (2, 1, 3)]
        if iteration == 1:
            pieces, weight_own, log_degree = call(
                project_first_kernel,
                "project1",
                [sds((16, KV, QB)), sds((1, CB)), sds((1, CB))],
                (pos, weight_log, *quarters),
            )
        else:
            pieces = call(
                project_kernel,
                f"project{iteration}",
                sds((16, KV, QB)),
                (weight_log, *quarters),
            )
        pieces = lax.all_to_all(pieces, ("y", "z"), 0, 0)
        vec, square, away = call(
            next_kernel,
            f"next{iteration}",
            [sds((2 * KV, NI), BF16), sds((KV, 128)), sds((KV, CB + 128))],
            (pos, *tile(), weight_i, pieces),
            scratch=[pltpu.VMEM((3 * KV, NI), BF16)],
        )
    total = call(
        core_add_kernel,
        "core_add",
        sds((KV, CB + 128)),
        (own_half(ITERS), from_core(away), square),
    )
    totals = [total] + [from_x(total, d) for d in (1, 3, 2)]
    proj, grams = call(
        last_kernel, "last", [sds((KV, CB)), sds((32, 8, 128))], (weight_own, *totals)
    )
    grams = lax.all_to_all(grams, ("z", "y", "c"), 0, 0)
    embedding, log_degree = call(
        finish_kernel, "finish", [sds((KV, CB)), sds((1, CB))], (proj, grams, log_degree)
    )
    return embedding, log_degree.reshape(CB)


def solution(mesh):
    grid = Mesh(mesh.devices.reshape(4, 4, 4, 2), ("x", "z", "y", "c"))
    col = ("z", "y", "c")
    in_specs = (P(col, None), P(col), P(None, col))
    out_specs = (P(None, col), P(col))
    return jax.shard_map(body, mesh=grid, in_specs=in_specs, out_specs=out_specs, check_vma=False)
```

```python
import functools
import math

import jax
import jax.numpy as jnp
from jax import lax
from jax.experimental import pallas as pl
from jax.experimental.pallas import tpu as pltpu
from jax.sharding import Mesh
from jax.sharding import PartitionSpec as P


ITERS = 3
F = 128
CB = 1024
QB = CB // 4
NJ = 2 * CB
NI = 16 * QB
KV = 16
NTOT = 32768
CLS = QB + 4 * KV
PROWS = CLS + 16
base_width = 2.8
width_growth = 1.3
F32 = jnp.float32
BF16 = jnp.bfloat16
VM = pltpu.VMEM
NN = (((1,), (0,)), ((), ()))
NT = (((1,), (1,)), ((), ()))
TN = (((0,), (0,)), ((), ()))


def dot(a, b, dims):
    return lax.dot_general(a, b, dims, preferred_element_type=F32)


def call(kernel, name, outs, args, flops=0, scratch=(), far=()):
    def spec(n, a):
        if a.dtype == jnp.int32 and a.ndim == 1:
            return pl.BlockSpec(memory_space=pltpu.SMEM)
        return pl.BlockSpec(memory_space=pltpu.HBM if n in far else VM)

    return pl.pallas_call(
        kernel,
        out_shape=outs,
        in_specs=[spec(n, a) for n, a in enumerate(args)],
        out_specs=jax.tree.map(lambda _: pl.BlockSpec(memory_space=VM), outs),
        scratch_shapes=scratch,
        compiler_params=pltpu.CompilerParams(vmem_limit_bytes=24 << 20),
        cost_estimate=pl.CostEstimate(flops=flops, bytes_accessed=0, transcendentals=0),
        name=name,
    )(*args)


def sds(shape, dtype=F32):
    return jax.ShapeDtypeStruct(shape, dtype)


def vmem(shape, dtype=F32):
    return pltpu.VMEM(shape, dtype)


def keep(a):
    return pltpu.with_memory_space_constraint(a, VM)


def pack_kernel(pos, frames, classes, start, piece, mine, quarter, own_classes, sems):
    x = pos[0]
    at = pl.multiple_of(pos[0] * QB, QB)
    copies = (
        pltpu.make_async_copy(frames.at[pl.ds(at, QB), :], piece.at[0:QB, :], sems.at[0]),
        pltpu.make_async_copy(start.at[:, pl.ds(at, QB)], quarter, sems.at[1]),
        pltpu.make_async_copy(classes, own_classes, sems.at[2]),
        pltpu.make_async_copy(frames, mine.at[0:CB, :], sems.at[3]),
    )
    for copy in copies:
        copy.start()
    for copy in copies:
        copy.wait()
    cls = own_classes[...].astype(F32)
    mine[CB:, :] = jnp.concatenate([cls, jnp.zeros_like(cls)], axis=0).astype(BF16)
    wide = piece[0:QB, :].astype(F32)
    square = wide * wide
    upper = square.astype(BF16)
    lower = (square - upper.astype(F32)).astype(BF16)
    ones = jnp.ones((8, F), BF16)
    half = -0.5 * (dot(ones, upper, NT) + dot(ones, lower, NT))[0:1]
    p1 = half.astype(BF16).astype(F32)
    p2 = (half - p1).astype(BF16).astype(F32)
    extra = [p[:, h * 128 : (h + 1) * 128] for p in (p1, p2, half - p1 - p2) for h in range(2)]
    extra.append(own_classes[pl.ds(2 * x, 1), :].astype(F32))
    extra.append(own_classes[pl.ds(2 * x + 1, 1), :].astype(F32))
    extra.append(jnp.ones((8, 128), F32))
    piece[CLS:PROWS, :] = jnp.concatenate(extra, axis=0).astype(BF16)
    high = quarter[...].astype(BF16)
    low = (quarter[...] - high.astype(F32)).astype(BF16)
    for h in range(2):
        at = QB + 2 * h * KV
        piece[at : at + KV, :] = high[:, h * 128 : (h + 1) * 128]
        piece[at + KV : at + 2 * KV, :] = low[:, h * 128 : (h + 1) * 128]


def stack_kernel(a, b, d, c, ready, out):
    del ready
    for n, ref in enumerate((a, b, c, d)):
        out[n] = ref[...]


def augment(rows):
    wide = rows.astype(F32)
    half = -0.5 * jnp.sum(wide * wide, axis=1, keepdims=True)
    p1 = half.astype(BF16).astype(F32)
    p2 = (half - p1).astype(BF16).astype(F32)
    lane = lax.broadcasted_iota(jnp.int32, (rows.shape[0], 128), 1)
    extra = jnp.where(lane < 3, 1.0, 0.0)
    for n, part in enumerate((p1, p2, half - p1 - p2)):
        extra = jnp.where(lane == 3 + n, part, extra)
    return jnp.concatenate([rows, extra.astype(BF16)], axis=1)


def inverse_width(cls):
    return jnp.exp2(cls * (-math.log2(width_growth))) * (1.0 / base_width)


def side_kernel(block, aug_j, coef_j):
    aug_j[...] = augment(block[0:CB, :])
    coef = inverse_width(block[CB:, :].astype(F32)) * (2.0 * math.log2(math.e))
    for r in range(8):
        coef_j[:, r * 128 : (r + 1) * 128] = coef[r : r + 1, :]


def spread(row, c, out):
    for quarter in range(4):
        lo = quarter * QB
        own, other = row[:, lo : lo + QB], row[:, CB + lo : CB + lo + QB]
        for core in range(2):
            value = jnp.where(c == core, own, other)
            for n in range(16):
                out[8 * n + 2 * quarter + core] = value


def rows_kernel(count, first, last, pos, *refs):
    groups, (aug_own, coef_own, aug_other, coef_other) = refs[:count], refs[count : count + 4]
    k_refs, out = refs[-1 - count : -1], refs[-1]
    row = lax.broadcasted_iota(jnp.int32, (16, 128), 0)
    lane = lax.broadcasted_iota(jnp.int32, (16, 128), 1)
    picks = []
    for h in range(2):
        parts = jnp.logical_and(lane < 3, row == 2 * lane + h)
        ones = jnp.logical_and(jnp.logical_and(lane >= 3, lane < 6), row == 8)
        cls = jnp.logical_and(lane == 8, row == 6 + h)
        pick = jnp.logical_or(jnp.logical_or(parts, ones), cls)
        picks.append(jnp.where(pick, 1.0, 0.0).astype(BF16))
    half = 512
    sides = ((0, aug_own, coef_own), (CB, aug_other, coef_other))
    totals = [
        jnp.zeros((8, CB), F32) if first else refs[count + 4][:, lo : lo + CB] for lo, _, _ in sides
    ]
    for pieces, k_ref in zip(groups, k_refs):
        for n in range(2):
            columns = [
                dot(pieces[m, CLS:PROWS, :], pick, TN) for m in (2 * n, 2 * n + 1) for pick in picks
            ]
            columns = jnp.concatenate(columns, axis=0)
            rows = jnp.concatenate([pieces[2 * n, 0:QB, :], pieces[2 * n + 1, 0:QB, :]], axis=0)
            aug_i = jnp.concatenate([rows, columns.astype(BF16)], axis=1)
            coef_i = inverse_width(columns[:, 8:9])
            for s, (lo, aug, coef) in enumerate(sides):
                e = jnp.exp2(dot(aug_i, aug[...], NT) * coef_i * coef[...])
                k_ref[n * half : (n + 1) * half, lo : lo + CB] = e.astype(BF16)
                totals[s] = totals[s] + jnp.sum(e.reshape(half // 8, 8, CB), axis=0)
    if last:
        total = jnp.concatenate(totals, axis=1)
        spread(jnp.sum(total, axis=0, keepdims=True), pos[1], out)
    else:
        for total, (lo, _, _) in zip(totals, sides):
            out[:, lo : lo + CB] = total


def side_i(pos, table, row):
    for n in range(16):
        at = pos[2 + n] * 8
        terms = [table[at + k] for k in range(8)]
        while len(terms) > 1:
            terms = [a + b for a, b in zip(terms[::2], terms[1::2])]
        row[:, n * QB : (n + 1) * QB] = terms[0]


def apply_k(v, ks, columns=slice(None)):
    n0 = NI // len(ks)
    terms = [dot(v[:, n * n0 : (n + 1) * n0], k[:, columns], NN) for n, k in enumerate(ks)]
    return (terms[0] + terms[1]) + (terms[2] + terms[3])


def degree_kernel(pos, k0, k1, k2, k3, table, dens_i, out):
    side_i(pos, table, dens_i)
    dens_i[...] = dens_i[...] * (1.0 / NTOT)
    inverse = jnp.broadcast_to(1.0 / dens_i[...], (8, NI)).astype(BF16)
    spread(apply_k(inverse, (k0, k1, k2, k3))[0:1], pos[1], out)


OWN, AWAY = slice(0, CB), slice(CB, NJ)


def first_kernel(
    pos, k0, k1, k2, k3, g0, g1, g2, g3, dens_i, table,
    vec, weight_i, weight_log, away, row,
):
    side_i(pos, table, row)
    row[...] = row[...] / (NTOT * dens_i[...])
    weight_i[...] = 1.0 / (dens_i[...] * jnp.sqrt(row[...]))
    weight_log[0:1, :] = weight_i[:, :QB]
    weight_log[1:2, :] = jnp.log(row[:, :QB])
    weight_log[2:, :] = jnp.zeros((6, QB), F32)
    for g, ref in enumerate((g0, g1, g2, g3)):
        for n in range(4):
            at = (4 * g + n) * QB
            for h in range(2):
                both = ref[n, QB + 2 * h * KV : QB + 2 * (h + 1) * KV, :].astype(F32)
                lo = at + h * 128
                part = (both[:KV] + both[KV:]) * weight_i[:, lo : lo + 128]
                vec[:, lo : lo + 128] = part.astype(BF16)
    away[...] = apply_k(vec, (k0, k1, k2, k3), AWAY)


def own_kernel(k0, k1, k2, k3, vec, own):
    y = apply_k(vec, (k0, k1, k2, k3), OWN)
    if vec.shape[0] == 2 * KV:
        y = y[:KV] + y[KV:]
    own[...] = y


def next_kernel(pos, k0, k1, k2, k3, weight_i, pieces, vec, gram, away, parts):
    for n in range(16):
        at = n * QB
        p = pieces[pos[2 + n]]
        v = p * weight_i[0:1, at : at + QB]
        hi = v.astype(BF16)
        vec[0:KV, at : at + QB] = hi
        vec[KV:, at : at + QB] = (v - hi.astype(F32)).astype(BF16)
        p1 = p.astype(BF16)
        r1 = p - p1.astype(F32)
        p2 = r1.astype(BF16)
        parts[0:KV, at : at + QB] = p1
        parts[KV : 2 * KV, at : at + QB] = p2
        parts[2 * KV :, at : at + QB] = (r1 - p2.astype(F32)).astype(BF16)
    s = dot(parts[...], parts[...], NT)
    rows = s[0:KV] + s[KV : 2 * KV] + s[2 * KV :]
    square = rows[:, 0:KV] + rows[:, KV : 2 * KV] + rows[:, 2 * KV :]
    square = jnp.concatenate([square, jnp.zeros((KV, 128 - KV), F32)], axis=1)
    gram[...] = square
    y2 = apply_k(vec, (k0, k1, k2, k3), AWAY)
    away[:, :CB] = y2[0:KV] + y2[KV:]
    away[:, CB:] = square


def core_sum_kernel(pos, own, away, *refs):
    outs = refs[-4:]
    for d, out in enumerate(outs):
        at = pl.ds(pl.multiple_of((pos[0] ^ d) * QB, QB), QB)
        out[:KV, :QB] = own[:, at] + away[:, at]
    if away.shape[1] > CB:
        gram = refs[0][...] + away[:, CB:]
        for ref in outs:
            ref[:, QB:] = gram
    else:
        for ref in outs:
            ref[KV:, :] = refs[0][...]


def core_add_kernel(own, away, gram, out):
    out[:, :CB] = own[...] + away[:, :CB]
    out[:, CB:] = gram[...] + away[:, CB:]


def eliminate(gram, y):
    row = lax.broadcasted_iota(jnp.int32, (KV, 128), 0)
    columns = [jnp.broadcast_to(gram[:, j : j + 1], (KV, 128)) for j in range(KV)]
    tiles = [y[:, lo : lo + 128] for lo in range(0, y.shape[1], 128)]
    pivots = jnp.zeros((KV, 128), F32)
    for k in range(KV):
        pivot = columns[k][k : k + 1, :]
        ratio = jnp.where(row > k, columns[k] * (1.0 / pivot), 0.0)
        pivots = jnp.where(row == k, pivot, pivots)
        for j in range(k + 1, KV):
            columns[j] = columns[j] - ratio * columns[j][k : k + 1, :]
        tiles = [tile - ratio * tile[k : k + 1, :] for tile in tiles]
    scale = 1.0 / jnp.sqrt(pivots)
    return jnp.concatenate([tile * scale for tile in tiles], axis=1)


def project_first_kernel(pos, weight_log, q0, q1, q2, q3, out, weight_own, log_degree):
    y = (q0[:KV] + q1[:KV]) + (q2[:KV] + q3[:KV])
    p = y * weight_log[0:1, :]
    for n in range(16):
        out[n] = p
    for d, ref in zip((0, 2, 1, 3), (q0, q1, q2, q3)):
        at = pl.ds(pl.multiple_of((pos[0] ^ d) * QB, QB), QB)
        weight_own[:, at] = ref[KV : KV + 1, :]
        log_degree[:, at] = ref[KV + 1 : KV + 2, :]


def project_kernel(weight_log, q0, q1, q2, q3, out):
    total = (q0[...] + q1[...]) + (q2[...] + q3[...])
    p = eliminate(total[:, QB:], total[:, :QB]) * weight_log[0:1, :]
    for n in range(16):
        out[n] = p


def last_kernel(weight_own, q0, q1, q2, q3, proj, grams):
    total = (q0[...] + q1[...]) + (q2[...] + q3[...])
    y = eliminate(total[:, CB:], total[:, :CB])
    p = y * weight_own[...]
    proj[...] = p
    gram = lax.dot_general(p, p, NT, precision=lax.Precision.HIGHEST, preferred_element_type=F32)
    gram = jnp.concatenate([gram[:8], gram[8:], jnp.zeros((8, 128 - 2 * KV), F32)], axis=1)
    for n in range(32):
        grams[n] = gram


def finish_kernel(proj, grams, log_in, out, log_degree):
    log_degree[...] = log_in[...]
    terms = [grams[n] for n in range(32)]
    while len(terms) > 1:
        terms = [a + b for a, b in zip(terms[::2], terms[1::2])]
    wide = terms[0]
    gram = jnp.concatenate([wide[:, :KV], wide[:, KV : 2 * KV]], axis=0)
    gram = jnp.concatenate([gram, jnp.zeros((KV, 128 - KV), F32)], axis=1)
    lane = lax.broadcasted_iota(jnp.int32, (KV, 128), 1)
    row = lax.broadcasted_iota(jnp.int32, (KV, 128), 0)
    factor = eliminate(gram, jnp.where(lane == row, math.sqrt(NTOT), 0.0))
    p = proj[...]
    terms = [factor[:, k : k + 1] * p[k : k + 1, :] for k in range(KV)]
    while len(terms) > 1:
        terms = [a + b for a, b in zip(terms[::2], terms[1::2])]
    out[...] = terms[0]


def device_number(x, z, y, c):
    return ((x * 4 + z) * 4 + y) * 2 + c


def shift(v, source):
    pairs = [
        (device_number(*source(x, z, y, c)), device_number(x, z, y, c))
        for x in range(4)
        for z in range(4)
        for y in range(4)
        for c in range(2)
    ]
    return lax.ppermute(v, ("x", "z", "y", "c"), pairs)


def from_line(v, d, second=False):
    def source(x, z, y, c):
        along_y = (c == 0) != second
        return (x, z, y ^ d, c) if along_y else (x, z ^ d, y, c)

    return shift(v, source)


def from_x(v, d):
    return shift(v, lambda x, z, y, c: (x ^ d, z, y, c))


def from_core(v):
    return shift(v, lambda x, z, y, c: (x, z, y, 1 - c))


def body(frames, width_class, start):
    x, z, y, c = (lax.axis_index(a) for a in ("x", "z", "y", "c"))
    second, first = jnp.arange(16, dtype=jnp.int32) // 4, jnp.arange(16, dtype=jnp.int32) % 4
    piece_y = y ^ jnp.where(c == 0, first, second)
    piece_z = z ^ jnp.where(c == 0, second, first)
    pos = jnp.concatenate([jnp.stack([x, c]), piece_y * 4 + piece_z]).astype(jnp.int32)

    classes = width_class.reshape(8, 128)
    piece, mine = call(
        pack_kernel,
        "pack",
        [sds((PROWS, F), BF16), vmem((CB + 16, F), BF16)],
        (pos, *(pltpu.with_memory_space_constraint(a, pltpu.HBM) for a in (frames, classes, start))),
        scratch=[
            pltpu.VMEM((KV, QB), F32),
            pltpu.VMEM((8, 128), jnp.int32),
            pltpu.SemaphoreType.DMA((4,)),
        ],
        far=(1, 2, 3),
    )
    line = [piece] + [from_line(piece, d) for d in (1, 3, 2)]
    shapes = [sds((CB, 2 * F), BF16), sds((1, CB))]
    own_side = call(side_kernel, "own_side", shapes, (keep(mine),), flops=CB * 4000)
    sides = own_side + call(
        side_kernel, "other_side", shapes, (from_core(keep(mine)),), flops=CB * 4000
    )
    line = call(
        stack_kernel, "stack", sds((4, PROWS, F), BF16), (*line, own_side[1])
    )
    groups = [line] + [from_line(line, d, True) for d in (1, 2, 3)]
    ks, sums = [None] * 4, ()
    for step in ((0,), (1,), (2,), (3,)):
        last = step == (3,)
        *made, total = call(
            functools.partial(rows_kernel, len(step), step == (0,), last),
            f"rows{step[0]}",
            [vmem((4 * QB, NJ), BF16)] * len(step) + [sds((128, 1, QB) if last else (8, NJ))],
            (pos, *(groups[g] for g in step), *sides, *sums),
            flops=len(step) * 4 * QB * NJ * 1024,
        )
        sums = (total,)
        for g, k in zip(step, made):
            ks[g] = k

    def tile():
        return [keep(k) for k in ks]

    everyone = ("y", "z", "x", "c")
    dens_i, table = call(
        degree_kernel,
        "degree",
        [sds((1, NI)), sds((128, 1, QB))],
        (pos, *tile(), lax.all_to_all(sums[0], everyone, 0, 0)),
    )
    vec, weight_i, weight_log, away = call(
        first_kernel,
        "first",
        [sds((KV, NI), BF16), sds((1, NI)), sds((8, QB)), sds((KV, CB))],
        (pos, *tile(), *groups, dens_i, lax.all_to_all(table, everyone, 0, 0)),
        scratch=[pltpu.VMEM((1, NI), F32)],
    )
    flops = 2 * NI * CB * 256

    def own_half(iteration):
        return call(own_kernel, f"own{iteration}", sds((KV, CB)), (*tile(), vec), flops=flops)

    for iteration in range(1, ITERS):
        shape = (KV + 8, QB) if iteration == 1 else (KV, QB + 128)
        quarters = call(
            core_sum_kernel,
            f"core_sum{iteration}",
            [sds(shape)] * 4,
            (pos, own_half(iteration), from_core(away), weight_log if iteration == 1 else square),
        )
        quarters = [quarters[0]] + [from_x(quarters[d], d) for d in (2, 1, 3)]
        if iteration == 1:
            pieces, weight_own, log_degree = call(
                project_first_kernel,
                "project1",
                [sds((16, KV, QB)), sds((1, CB)), sds((1, CB))],
                (pos, weight_log, *quarters),
            )
        else:
            pieces = call(
                project_kernel,
                f"project{iteration}",
                sds((16, KV, QB)),
                (weight_log, *quarters),
            )
        pieces = lax.all_to_all(pieces, ("y", "z"), 0, 0)
        vec, square, away = call(
            next_kernel,
            f"next{iteration}",
            [sds((2 * KV, NI), BF16), sds((KV, 128)), sds((KV, CB + 128))],
            (pos, *tile(), weight_i, pieces),
            scratch=[pltpu.VMEM((3 * KV, NI), BF16)],
        )
    total = call(
        core_add_kernel,
        "core_add",
        sds((KV, CB + 128)),
        (own_half(ITERS), from_core(away), square),
    )
    totals = [total] + [from_x(total, d) for d in (1, 3, 2)]
    proj, grams = call(
        last_kernel, "last", [sds((KV, CB)), sds((32, 8, 128))], (weight_own, *totals)
    )
    grams = lax.all_to_all(grams, ("z", "y", "c"), 0, 0)
    embedding, log_degree = call(
        finish_kernel, "finish", [sds((KV, CB)), sds((1, CB))], (proj, grams, log_degree)
    )
    return embedding, log_degree.reshape(CB)


def solution(mesh):
    grid = Mesh(mesh.devices.reshape(4, 4, 4, 2), ("x", "z", "y", "c"))
    col = ("z", "y", "c")
    in_specs = (P(col, None), P(col), P(None, col))
    out_specs = (P(None, col), P(col))
    return jax.shard_map(body, mesh=grid, in_specs=in_specs, out_specs=out_specs, check_vma=False)
```

```python
import functools
import math

import jax
import jax.numpy as jnp
from jax import lax
from jax.experimental import pallas as pl
from jax.experimental.pallas import tpu as pltpu
from jax.sharding import Mesh
from jax.sharding import PartitionSpec as P


ITERS = 3
F = 128
CB = 1024
QB = CB // 4
NJ = 2 * CB
NI = 16 * QB
KV = 16
NTOT = 32768
CLS = QB + 4 * KV
PROWS = CLS + 16
base_width = 2.8
width_growth = 1.3
F32 = jnp.float32
BF16 = jnp.bfloat16
VM = pltpu.VMEM
NN = (((1,), (0,)), ((), ()))
NT = (((1,), (1,)), ((), ()))
TN = (((0,), (0,)), ((), ()))


def dot(a, b, dims):
    return lax.dot_general(a, b, dims, preferred_element_type=F32)


def call(kernel, name, outs, args, flops=0, scratch=(), far=()):
    def spec(n, a):
        if a.dtype == jnp.int32 and a.ndim == 1:
            return pl.BlockSpec(memory_space=pltpu.SMEM)
        return pl.BlockSpec(memory_space=pltpu.HBM if n in far else VM)

    return pl.pallas_call(
        kernel,
        out_shape=outs,
        in_specs=[spec(n, a) for n, a in enumerate(args)],
        out_specs=jax.tree.map(lambda _: pl.BlockSpec(memory_space=VM), outs),
        scratch_shapes=scratch,
        compiler_params=pltpu.CompilerParams(vmem_limit_bytes=24 << 20),
        cost_estimate=pl.CostEstimate(flops=flops, bytes_accessed=0, transcendentals=0),
        name=name,
    )(*args)


def sds(shape, dtype=F32):
    return jax.ShapeDtypeStruct(shape, dtype)


def vmem(shape, dtype=F32):
    return pltpu.VMEM(shape, dtype)


def keep(a):
    return pltpu.with_memory_space_constraint(a, VM)


def pack_kernel(pos, frames, classes, start, piece, mine, quarter, own_classes, sems):
    x = pos[0]
    at = pl.multiple_of(pos[0] * QB, QB)
    copies = (
        pltpu.make_async_copy(frames.at[pl.ds(at, QB), :], piece.at[0:QB, :], sems.at[0]),
        pltpu.make_async_copy(start.at[:, pl.ds(at, QB)], quarter, sems.at[1]),
        pltpu.make_async_copy(classes, own_classes, sems.at[2]),
        pltpu.make_async_copy(frames, mine.at[0:CB, :], sems.at[3]),
    )
    for copy in copies:
        copy.start()
    copies[2].wait()
    copies[0].wait()
    cls = own_classes[...].astype(F32)
    mine[CB:, :] = jnp.concatenate([cls, jnp.zeros_like(cls)], axis=0).astype(BF16)
    wide = piece[0:QB, :].astype(F32)
    square = wide * wide
    upper = square.astype(BF16)
    lower = (square - upper.astype(F32)).astype(BF16)
    ones = jnp.ones((8, F), BF16)
    half = -0.5 * (dot(ones, upper, NT) + dot(ones, lower, NT))[0:1]
    p1 = half.astype(BF16).astype(F32)
    p2 = (half - p1).astype(BF16).astype(F32)
    extra = [p[:, h * 128 : (h + 1) * 128] for p in (p1, p2, half - p1 - p2) for h in range(2)]
    extra.append(own_classes[pl.ds(2 * x, 1), :].astype(F32))
    extra.append(own_classes[pl.ds(2 * x + 1, 1), :].astype(F32))
    extra.append(jnp.ones((8, 128), F32))
    piece[CLS:PROWS, :] = jnp.concatenate(extra, axis=0).astype(BF16)
    copies[1].wait()
    high = quarter[...].astype(BF16)
    low = (quarter[...] - high.astype(F32)).astype(BF16)
    for h in range(2):
        at = QB + 2 * h * KV
        piece[at : at + KV, :] = high[:, h * 128 : (h + 1) * 128]
        piece[at + KV : at + 2 * KV, :] = low[:, h * 128 : (h + 1) * 128]
    copies[3].wait()


def stack_kernel(a, b, d, c, ready, out):
    del ready
    for n, ref in enumerate((a, b, c, d)):
        out[n] = ref[...]


def augment(rows):
    wide = rows.astype(F32)
    half = -0.5 * jnp.sum(wide * wide, axis=1, keepdims=True)
    p1 = half.astype(BF16).astype(F32)
    p2 = (half - p1).astype(BF16).astype(F32)
    lane = lax.broadcasted_iota(jnp.int32, (rows.shape[0], 128), 1)
    extra = jnp.where(lane < 3, 1.0, 0.0)
    for n, part in enumerate((p1, p2, half - p1 - p2)):
        extra = jnp.where(lane == 3 + n, part, extra)
    return jnp.concatenate([rows, extra.astype(BF16)], axis=1)


def inverse_width(cls):
    return jnp.exp2(cls * (-math.log2(width_growth))) * (1.0 / base_width)


def side_kernel(block, aug_j, coef_j):
    aug_j[...] = augment(block[0:CB, :])
    coef = inverse_width(block[CB:, :].astype(F32)) * (2.0 * math.log2(math.e))
    for r in range(8):
        coef_j[:, r * 128 : (r + 1) * 128] = coef[r : r + 1, :]


def spread(row, c, out):
    for quarter in range(4):
        lo = quarter * QB
        own, other = row[:, lo : lo + QB], row[:, CB + lo : CB + lo + QB]
        for core in range(2):
            value = jnp.where(c == core, own, other)
            for n in range(16):
                out[8 * n + 2 * quarter + core] = value


def rows_kernel(count, first, last, pos, *refs):
    groups, (aug_own, coef_own, aug_other, coef_other) = refs[:count], refs[count : count + 4]
    k_refs, out = refs[-1 - count : -1], refs[-1]
    row = lax.broadcasted_iota(jnp.int32, (16, 128), 0)
    lane = lax.broadcasted_iota(jnp.int32, (16, 128), 1)
    picks = []
    for h in range(2):
        parts = jnp.logical_and(lane < 3, row == 2 * lane + h)
        ones = jnp.logical_and(jnp.logical_and(lane >= 3, lane < 6), row == 8)
        cls = jnp.logical_and(lane == 8, row == 6 + h)
        pick = jnp.logical_or(jnp.logical_or(parts, ones), cls)
        picks.append(jnp.where(pick, 1.0, 0.0).astype(BF16))
    half = 512
    sides = ((0, aug_own, coef_own), (CB, aug_other, coef_other))
    totals = [
        jnp.zeros((8, CB), F32) if first else refs[count + 4][:, lo : lo + CB] for lo, _, _ in sides
    ]
    for pieces, k_ref in zip(groups, k_refs):
        for n in range(2):
            columns = [
                dot(pieces[m, CLS:PROWS, :], pick, TN) for m in (2 * n, 2 * n + 1) for pick in picks
            ]
            columns = jnp.concatenate(columns, axis=0)
            rows = jnp.concatenate([pieces[2 * n, 0:QB, :], pieces[2 * n + 1, 0:QB, :]], axis=0)
            aug_i = jnp.concatenate([rows, columns.astype(BF16)], axis=1)
            coef_i = inverse_width(columns[:, 8:9])
            for s, (lo, aug, coef) in enumerate(sides):
                e = jnp.exp2(dot(aug_i, aug[...], NT) * coef_i * coef[...])
                k_ref[n * half : (n + 1) * half, lo : lo + CB] = e.astype(BF16)
                totals[s] = totals[s] + jnp.sum(e.reshape(half // 8, 8, CB), axis=0)
    if last:
        total = jnp.concatenate(totals, axis=1)
        spread(jnp.sum(total, axis=0, keepdims=True), pos[1], out)
    else:
        for total, (lo, _, _) in zip(totals, sides):
            out[:, lo : lo + CB] = total


def side_i(pos, table, row):
    for n in range(16):
        at = pos[2 + n] * 8
        terms = [table[at + k] for k in range(8)]
        while len(terms) > 1:
            terms = [a + b for a, b in zip(terms[::2], terms[1::2])]
        row[:, n * QB : (n + 1) * QB] = terms[0]


def apply_k(v, ks, columns=slice(None)):
    n0 = NI // len(ks)
    terms = [dot(v[:, n * n0 : (n + 1) * n0], k[:, columns], NN) for n, k in enumerate(ks)]
    return (terms[0] + terms[1]) + (terms[2] + terms[3])


def degree_kernel(pos, k0, k1, k2, k3, table, dens_i, out):
    side_i(pos, table, dens_i)
    dens_i[...] = dens_i[...] * (1.0 / NTOT)
    inverse = jnp.broadcast_to(1.0 / dens_i[...], (8, NI)).astype(BF16)
    spread(apply_k(inverse, (k0, k1, k2, k3))[0:1], pos[1], out)


OWN, AWAY = slice(0, CB), slice(CB, NJ)


def first_kernel(
    pos, k0, k1, k2, k3, g0, g1, g2, g3, dens_i, table,
    vec, weight_i, weight_log, away, row,
):
    side_i(pos, table, row)
    row[...] = row[...] / (NTOT * dens_i[...])
    weight_i[...] = 1.0 / (dens_i[...] * jnp.sqrt(row[...]))
    weight_log[0:1, :] = weight_i[:, :QB]
    weight_log[1:2, :] = jnp.log(row[:, :QB])
    weight_log[2:, :] = jnp.zeros((6, QB), F32)
    for g, ref in enumerate((g0, g1, g2, g3)):
        for n in range(4):
            at = (4 * g + n) * QB
            for h in range(2):
                both = ref[n, QB + 2 * h * KV : QB + 2 * (h + 1) * KV, :].astype(F32)
                lo = at + h * 128
                part = (both[:KV] + both[KV:]) * weight_i[:, lo : lo + 128]
                vec[:, lo : lo + 128] = part.astype(BF16)
    away[...] = apply_k(vec, (k0, k1, k2, k3), AWAY)


def own_kernel(k0, k1, k2, k3, vec, own):
    y = apply_k(vec, (k0, k1, k2, k3), OWN)
    if vec.shape[0] == 2 * KV:
        y = y[:KV] + y[KV:]
    own[...] = y


def next_kernel(pos, k0, k1, k2, k3, weight_i, pieces, vec, gram, away, parts):
    for n in range(16):
        at = n * QB
        p = pieces[pos[2 + n]]
        v = p * weight_i[0:1, at : at + QB]
        hi = v.astype(BF16)
        vec[0:KV, at : at + QB] = hi
        vec[KV:, at : at + QB] = (v - hi.astype(F32)).astype(BF16)
        p1 = p.astype(BF16)
        r1 = p - p1.astype(F32)
        p2 = r1.astype(BF16)
        parts[0:KV, at : at + QB] = p1
        parts[KV : 2 * KV, at : at + QB] = p2
        parts[2 * KV :, at : at + QB] = (r1 - p2.astype(F32)).astype(BF16)
    s = dot(parts[...], parts[...], NT)
    rows = s[0:KV] + s[KV : 2 * KV] + s[2 * KV :]
    square = rows[:, 0:KV] + rows[:, KV : 2 * KV] + rows[:, 2 * KV :]
    square = jnp.concatenate([square, jnp.zeros((KV, 128 - KV), F32)], axis=1)
    gram[...] = square
    y2 = apply_k(vec, (k0, k1, k2, k3), AWAY)
    away[:, :CB] = y2[0:KV] + y2[KV:]
    away[:, CB:] = square


def core_sum_kernel(pos, own, away, *refs):
    outs = refs[-4:]
    for d, out in enumerate(outs):
        at = pl.ds(pl.multiple_of((pos[0] ^ d) * QB, QB), QB)
        out[:KV, :QB] = own[:, at] + away[:, at]
    if away.shape[1] > CB:
        gram = refs[0][...] + away[:, CB:]
        for ref in outs:
            ref[:, QB:] = gram
    else:
        for ref in outs:
            ref[KV:, :] = refs[0][...]


def core_add_kernel(own, away, gram, out):
    out[:, :CB] = own[...] + away[:, :CB]
    out[:, CB:] = gram[...] + away[:, CB:]


def eliminate(gram, y):
    row = lax.broadcasted_iota(jnp.int32, (KV, 128), 0)
    columns = [jnp.broadcast_to(gram[:, j : j + 1], (KV, 128)) for j in range(KV)]
    tiles = [y[:, lo : lo + 128] for lo in range(0, y.shape[1], 128)]
    pivots = jnp.zeros((KV, 128), F32)
    for k in range(KV):
        pivot = columns[k][k : k + 1, :]
        ratio = jnp.where(row > k, columns[k] * (1.0 / pivot), 0.0)
        pivots = jnp.where(row == k, pivot, pivots)
        for j in range(k + 1, KV):
            columns[j] = columns[j] - ratio * columns[j][k : k + 1, :]
        tiles = [tile - ratio * tile[k : k + 1, :] for tile in tiles]
    scale = 1.0 / jnp.sqrt(pivots)
    return jnp.concatenate([tile * scale for tile in tiles], axis=1)


def project_first_kernel(pos, weight_log, q0, q1, q2, q3, out, weight_own, log_degree):
    y = (q0[:KV] + q1[:KV]) + (q2[:KV] + q3[:KV])
    p = y * weight_log[0:1, :]
    for n in range(16):
        out[n] = p
    for d, ref in zip((0, 2, 1, 3), (q0, q1, q2, q3)):
        at = pl.ds(pl.multiple_of((pos[0] ^ d) * QB, QB), QB)
        weight_own[:, at] = ref[KV : KV + 1, :]
        log_degree[:, at] = ref[KV + 1 : KV + 2, :]


def project_kernel(weight_log, q0, q1, q2, q3, out):
    total = (q0[...] + q1[...]) + (q2[...] + q3[...])
    p = eliminate(total[:, QB:], total[:, :QB]) * weight_log[0:1, :]
    for n in range(16):
        out[n] = p


def last_kernel(weight_own, q0, q1, q2, q3, proj, grams):
    total = (q0[...] + q1[...]) + (q2[...] + q3[...])
    y = eliminate(total[:, CB:], total[:, :CB])
    p = y * weight_own[...]
    proj[...] = p
    gram = lax.dot_general(p, p, NT, precision=lax.Precision.HIGHEST, preferred_element_type=F32)
    gram = jnp.concatenate([gram[k : k + 1] for k in range(KV)], axis=1)
    for n in range(32):
        grams[n] = gram


def finish_kernel(proj, grams, log_in, out, log_degree):
    log_degree[...] = log_in[...]
    terms = [grams[n] for n in range(32)]
    while len(terms) > 1:
        terms = [a + b for a, b in zip(terms[::2], terms[1::2])]
    wide = terms[0]
    gram = jnp.concatenate([wide[:, k * KV : (k + 1) * KV] for k in range(KV)], axis=0)
    gram = jnp.concatenate([gram, jnp.zeros((KV, 128 - KV), F32)], axis=1)
    lane = lax.broadcasted_iota(jnp.int32, (KV, 128), 1)
    row = lax.broadcasted_iota(jnp.int32, (KV, 128), 0)
    factor = eliminate(gram, jnp.where(lane == row, math.sqrt(NTOT), 0.0))
    p = proj[...]
    terms = [factor[:, k : k + 1] * p[k : k + 1, :] for k in range(KV)]
    while len(terms) > 1:
        terms = [a + b for a, b in zip(terms[::2], terms[1::2])]
    out[...] = terms[0]


def device_number(x, z, y, c):
    return ((x * 4 + z) * 4 + y) * 2 + c


def shift(v, source):
    pairs = [
        (device_number(*source(x, z, y, c)), device_number(x, z, y, c))
        for x in range(4)
        for z in range(4)
        for y in range(4)
        for c in range(2)
    ]
    return lax.ppermute(v, ("x", "z", "y", "c"), pairs)


def from_line(v, d, second=False):
    def source(x, z, y, c):
        along_y = (c == 0) != second
        return (x, z, y ^ d, c) if along_y else (x, z ^ d, y, c)

    return shift(v, source)


def from_x(v, d):
    return shift(v, lambda x, z, y, c: (x ^ d, z, y, c))


def from_core(v):
    return shift(v, lambda x, z, y, c: (x, z, y, 1 - c))


def body(frames, width_class, start):
    x, z, y, c = (lax.axis_index(a) for a in ("x", "z", "y", "c"))
    second, first = jnp.arange(16, dtype=jnp.int32) // 4, jnp.arange(16, dtype=jnp.int32) % 4
    piece_y = y ^ jnp.where(c == 0, first, second)
    piece_z = z ^ jnp.where(c == 0, second, first)
    pos = jnp.concatenate([jnp.stack([x, c]), piece_y * 4 + piece_z]).astype(jnp.int32)

    classes = width_class.reshape(8, 128)
    piece, mine = call(
        pack_kernel,
        "pack",
        [sds((PROWS, F), BF16), vmem((CB + 16, F), BF16)],
        (pos, *(pltpu.with_memory_space_constraint(a, pltpu.HBM) for a in (frames, classes, start))),
        scratch=[
            pltpu.VMEM((KV, QB), F32),
            pltpu.VMEM((8, 128), jnp.int32),
            pltpu.SemaphoreType.DMA((4,)),
        ],
        far=(1, 2, 3),
    )
    line = [piece] + [from_line(piece, d) for d in (1, 3, 2)]
    shapes = [sds((CB, 2 * F), BF16), sds((1, CB))]
    own_side = call(side_kernel, "own_side", shapes, (keep(mine),), flops=CB * 4000)
    sides = own_side + call(
        side_kernel, "other_side", shapes, (from_core(keep(mine)),), flops=CB * 4000
    )
    line = call(
        stack_kernel, "stack", sds((4, PROWS, F), BF16), (*line, own_side[1])
    )
    groups = [line] + [from_line(line, d, True) for d in (1, 2, 3)]
    ks, sums = [None] * 4, ()
    for step in ((0,), (1,), (2,), (3,)):
        last = step == (3,)
        *made, total = call(
            functools.partial(rows_kernel, len(step), step == (0,), last),
            f"rows{step[0]}",
            [vmem((4 * QB, NJ), BF16)] * len(step) + [sds((128, 1, QB) if last else (8, NJ))],
            (pos, *(groups[g] for g in step), *sides, *sums),
            flops=len(step) * 4 * QB * NJ * 1024,
        )
        sums = (total,)
        for g, k in zip(step, made):
            ks[g] = k

    def tile():
        return [keep(k) for k in ks]

    everyone = ("y", "z", "x", "c")
    dens_i, table = call(
        degree_kernel,
        "degree",
        [sds((1, NI)), sds((128, 1, QB))],
        (pos, *tile(), lax.all_to_all(sums[0], everyone, 0, 0)),
    )
    vec, weight_i, weight_log, away = call(
        first_kernel,
        "first",
        [sds((KV, NI), BF16), sds((1, NI)), sds((8, QB)), sds((KV, CB))],
        (pos, *tile(), *groups, dens_i, lax.all_to_all(table, everyone, 0, 0)),
        scratch=[pltpu.VMEM((1, NI), F32)],
    )
    flops = 2 * NI * CB * 256

    def own_half(iteration):
        return call(own_kernel, f"own{iteration}", sds((KV, CB)), (*tile(), vec), flops=flops)

    for iteration in range(1, ITERS):
        shape = (KV + 8, QB) if iteration == 1 else (KV, QB + 128)
        quarters = call(
            core_sum_kernel,
            f"core_sum{iteration}",
            [sds(shape)] * 4,
            (pos, own_half(iteration), from_core(away), weight_log if iteration == 1 else square),
        )
        quarters = [quarters[0]] + [from_x(quarters[d], d) for d in (2, 1, 3)]
        if iteration == 1:
            pieces, weight_own, log_degree = call(
                project_first_kernel,
                "project1",
                [sds((16, KV, QB)), sds((1, CB)), sds((1, CB))],
                (pos, weight_log, *quarters),
            )
        else:
            pieces = call(
                project_kernel,
                f"project{iteration}",
                sds((16, KV, QB)),
                (weight_log, *quarters),
            )
        pieces = lax.all_to_all(pieces, ("y", "z"), 0, 0)
        vec, square, away = call(
            next_kernel,
            f"next{iteration}",
            [sds((2 * KV, NI), BF16), sds((KV, 128)), sds((KV, CB + 128))],
            (pos, *tile(), weight_i, pieces),
            scratch=[pltpu.VMEM((3 * KV, NI), BF16)],
        )
    total = call(
        core_add_kernel,
        "core_add",
        sds((KV, CB + 128)),
        (own_half(ITERS), from_core(away), square),
    )
    totals = [total] + [from_x(total, d) for d in (1, 3, 2)]
    proj, grams = call(
        last_kernel, "last", [sds((KV, CB)), sds((32, 1, KV * KV))], (weight_own, *totals)
    )
    grams = lax.all_to_all(grams, ("z", "y", "c"), 0, 0)
    embedding, log_degree = call(
        finish_kernel, "finish", [sds((KV, CB)), sds((1, CB))], (proj, grams, log_degree)
    )
    return embedding, log_degree.reshape(CB)


def solution(mesh):
    grid = Mesh(mesh.devices.reshape(4, 4, 4, 2), ("x", "z", "y", "c"))
    col = ("z", "y", "c")
    in_specs = (P(col, None), P(col), P(None, col))
    out_specs = (P(None, col), P(col))
    return jax.shard_map(body, mesh=grid, in_specs=in_specs, out_specs=out_specs, check_vma=False)
```

```python
import functools
import math

import jax
import jax.numpy as jnp
from jax import lax
from jax.experimental import pallas as pl
from jax.experimental.pallas import tpu as pltpu
from jax.sharding import Mesh
from jax.sharding import PartitionSpec as P


ITERS = 3
F = 128
CB = 1024
QB = CB // 4
NJ = 2 * CB
NI = 16 * QB
KV = 16
NTOT = 32768
CLS = QB + 4 * KV
PROWS = CLS + 16
base_width = 2.8
width_growth = 1.3
F32 = jnp.float32
BF16 = jnp.bfloat16
VM = pltpu.VMEM
NN = (((1,), (0,)), ((), ()))
NT = (((1,), (1,)), ((), ()))
TN = (((0,), (0,)), ((), ()))


def dot(a, b, dims):
    return lax.dot_general(a, b, dims, preferred_element_type=F32)


def call(kernel, name, outs, args, flops=0, scratch=(), far=()):
    def spec(n, a):
        if a.dtype == jnp.int32 and a.ndim == 1:
            return pl.BlockSpec(memory_space=pltpu.SMEM)
        return pl.BlockSpec(memory_space=pltpu.HBM if n in far else VM)

    return pl.pallas_call(
        kernel,
        out_shape=outs,
        in_specs=[spec(n, a) for n, a in enumerate(args)],
        out_specs=jax.tree.map(lambda _: pl.BlockSpec(memory_space=VM), outs),
        scratch_shapes=scratch,
        compiler_params=pltpu.CompilerParams(vmem_limit_bytes=24 << 20),
        cost_estimate=pl.CostEstimate(flops=flops, bytes_accessed=0, transcendentals=0),
        name=name,
    )(*args)


def sds(shape, dtype=F32):
    return jax.ShapeDtypeStruct(shape, dtype)


def vmem(shape, dtype=F32):
    return pltpu.VMEM(shape, dtype)


def keep(a):
    return pltpu.with_memory_space_constraint(a, VM)


def pack_kernel(pos, frames, classes, start, piece, mine, quarter, own_classes, sems):
    x = pos[0]
    at = pl.multiple_of(pos[0] * QB, QB)
    copies = (
        pltpu.make_async_copy(frames.at[pl.ds(at, QB), :], piece.at[0:QB, :], sems.at[0]),
        pltpu.make_async_copy(start.at[:, pl.ds(at, QB)], quarter, sems.at[1]),
        pltpu.make_async_copy(classes, own_classes, sems.at[2]),
        pltpu.make_async_copy(frames, mine.at[0:CB, :], sems.at[3]),
    )
    for copy in copies:
        copy.start()
    copies[2].wait()
    copies[0].wait()
    cls = own_classes[...].astype(F32)
    mine[CB:, :] = jnp.concatenate([cls, jnp.zeros_like(cls)], axis=0).astype(BF16)
    wide = piece[0:QB, :].astype(F32)
    square = wide * wide
    upper = square.astype(BF16)
    lower = (square - upper.astype(F32)).astype(BF16)
    ones = jnp.ones((8, F), BF16)
    half = -0.5 * (dot(ones, upper, NT) + dot(ones, lower, NT))[0:1]
    p1 = half.astype(BF16).astype(F32)
    p2 = (half - p1).astype(BF16).astype(F32)
    extra = [p[:, h * 128 : (h + 1) * 128] for p in (p1, p2, half - p1 - p2) for h in range(2)]
    extra.append(own_classes[pl.ds(2 * x, 1), :].astype(F32))
    extra.append(own_classes[pl.ds(2 * x + 1, 1), :].astype(F32))
    extra.append(jnp.ones((8, 128), F32))
    piece[CLS:PROWS, :] = jnp.concatenate(extra, axis=0).astype(BF16)
    copies[1].wait()
    high = quarter[...].astype(BF16)
    low = (quarter[...] - high.astype(F32)).astype(BF16)
    for h in range(2):
        at = QB + 2 * h * KV
        piece[at : at + KV, :] = high[:, h * 128 : (h + 1) * 128]
        piece[at + KV : at + 2 * KV, :] = low[:, h * 128 : (h + 1) * 128]
    copies[3].wait()


def stack_kernel(a, b, d, c, ready, out):
    del ready
    for n, ref in enumerate((a, b, c, d)):
        out[n] = ref[...]


def augment(rows):
    wide = rows.astype(F32)
    half = -0.5 * jnp.sum(wide * wide, axis=1, keepdims=True)
    p1 = half.astype(BF16).astype(F32)
    p2 = (half - p1).astype(BF16).astype(F32)
    lane = lax.broadcasted_iota(jnp.int32, (rows.shape[0], 128), 1)
    extra = jnp.where(lane < 3, 1.0, 0.0)
    for n, part in enumerate((p1, p2, half - p1 - p2)):
        extra = jnp.where(lane == 3 + n, part, extra)
    return jnp.concatenate([rows, extra.astype(BF16)], axis=1)


def inverse_width(cls):
    return jnp.exp2(cls * (-math.log2(width_growth))) * (1.0 / base_width)


def side_kernel(block, aug_j, coef_j):
    aug_j[...] = augment(block[0:CB, :])
    coef = inverse_width(block[CB:, :].astype(F32)) * (2.0 * math.log2(math.e))
    for r in range(8):
        coef_j[:, r * 128 : (r + 1) * 128] = coef[r : r + 1, :]


def spread(row, c, out):
    for quarter in range(4):
        lo = quarter * QB
        own, other = row[:, lo : lo + QB], row[:, CB + lo : CB + lo + QB]
        for core in range(2):
            value = jnp.where(c == core, own, other)
            for n in range(16):
                out[8 * n + 2 * quarter + core] = value


def rows_kernel(count, first, last, pos, *refs):
    groups, (aug_own, coef_own, aug_other, coef_other) = refs[:count], refs[count : count + 4]
    k_refs, out = refs[-1 - count : -1], refs[-1]
    row = lax.broadcasted_iota(jnp.int32, (16, 128), 0)
    lane = lax.broadcasted_iota(jnp.int32, (16, 128), 1)
    picks = []
    for h in range(2):
        parts = jnp.logical_and(lane < 3, row == 2 * lane + h)
        ones = jnp.logical_and(jnp.logical_and(lane >= 3, lane < 6), row == 8)
        cls = jnp.logical_and(lane == 8, row == 6 + h)
        pick = jnp.logical_or(jnp.logical_or(parts, ones), cls)
        picks.append(jnp.where(pick, 1.0, 0.0).astype(BF16))
    half = 512
    sides = ((0, aug_own, coef_own), (CB, aug_other, coef_other))
    totals = [
        jnp.zeros((8, CB), F32) if first else refs[count + 4][:, lo : lo + CB] for lo, _, _ in sides
    ]
    for pieces, k_ref in zip(groups, k_refs):
        for n in range(2):
            columns = [
                dot(pieces[m, CLS:PROWS, :], pick, TN) for m in (2 * n, 2 * n + 1) for pick in picks
            ]
            columns = jnp.concatenate(columns, axis=0)
            rows = jnp.concatenate([pieces[2 * n, 0:QB, :], pieces[2 * n + 1, 0:QB, :]], axis=0)
            aug_i = jnp.concatenate([rows, columns.astype(BF16)], axis=1)
            coef_i = inverse_width(columns[:, 8:9])
            for s, (lo, aug, coef) in enumerate(sides):
                e = jnp.exp2(dot(aug_i, aug[...], NT) * coef_i * coef[...])
                k_ref[n * half : (n + 1) * half, lo : lo + CB] = e.astype(BF16)
                totals[s] = totals[s] + jnp.sum(e.reshape(half // 8, 8, CB), axis=0)
    if last:
        total = jnp.concatenate(totals, axis=1)
        spread(jnp.sum(total, axis=0, keepdims=True), pos[1], out)
    else:
        for total, (lo, _, _) in zip(totals, sides):
            out[:, lo : lo + CB] = total


def side_i(pos, table, row):
    for n in range(16):
        at = pos[2 + n] * 8
        terms = [table[at + k] for k in range(8)]
        while len(terms) > 1:
            terms = [a + b for a, b in zip(terms[::2], terms[1::2])]
        row[:, n * QB : (n + 1) * QB] = terms[0]


def apply_k(v, ks, columns=slice(None)):
    n0 = NI // len(ks)
    terms = [dot(v[:, n * n0 : (n + 1) * n0], k[:, columns], NN) for n, k in enumerate(ks)]
    return (terms[0] + terms[1]) + (terms[2] + terms[3])


def degree_kernel(pos, k0, k1, k2, k3, table, dens_i, out):
    side_i(pos, table, dens_i)
    dens_i[...] = dens_i[...] * (1.0 / NTOT)
    inverse = jnp.broadcast_to(1.0 / dens_i[...], (8, NI)).astype(BF16)
    spread(apply_k(inverse, (k0, k1, k2, k3))[0:1], pos[1], out)


OWN, AWAY = slice(0, CB), slice(CB, NJ)


def first_kernel(
    pos, k0, k1, k2, k3, g0, g1, g2, g3, dens_i, table,
    vec, weight_i, weight_log, away, row,
):
    side_i(pos, table, row)
    row[...] = row[...] / (NTOT * dens_i[...])
    weight_i[...] = 1.0 / (dens_i[...] * jnp.sqrt(row[...]))
    weight_log[0:1, :] = weight_i[:, :QB]
    weight_log[1:2, :] = jnp.log(row[:, :QB])
    weight_log[2:, :] = jnp.zeros((6, QB), F32)
    for g, ref in enumerate((g0, g1, g2, g3)):
        for n in range(4):
            at = (4 * g + n) * QB
            for h in range(2):
                both = ref[n, QB + 2 * h * KV : QB + 2 * (h + 1) * KV, :].astype(F32)
                lo = at + h * 128
                part = (both[:KV] + both[KV:]) * weight_i[:, lo : lo + 128]
                vec[:, lo : lo + 128] = part.astype(BF16)
    away[...] = apply_k(vec, (k0, k1, k2, k3), AWAY)


def own_kernel(k0, k1, k2, k3, vec, own):
    y = apply_k(vec, (k0, k1, k2, k3), OWN)
    if vec.shape[0] == 2 * KV:
        y = y[:KV] + y[KV:]
    own[...] = y


def next_kernel(pos, k0, k1, k2, k3, weight_i, pieces, vec, gram, away, parts):
    for n in range(16):
        at = n * QB
        p = pieces[pos[2 + n]]
        v = p * weight_i[0:1, at : at + QB]
        hi = v.astype(BF16)
        vec[0:KV, at : at + QB] = hi
        vec[KV:, at : at + QB] = (v - hi.astype(F32)).astype(BF16)
        p1 = p.astype(BF16)
        r1 = p - p1.astype(F32)
        p2 = r1.astype(BF16)
        parts[0:KV, at : at + QB] = p1
        parts[KV : 2 * KV, at : at + QB] = p2
        parts[2 * KV :, at : at + QB] = (r1 - p2.astype(F32)).astype(BF16)
    s = dot(parts[...], parts[...], NT)
    rows = s[0:KV] + s[KV : 2 * KV] + s[2 * KV :]
    square = rows[:, 0:KV] + rows[:, KV : 2 * KV] + rows[:, 2 * KV :]
    square = jnp.concatenate([square, jnp.zeros((KV, 128 - KV), F32)], axis=1)
    gram[...] = square
    y2 = apply_k(vec, (k0, k1, k2, k3), AWAY)
    away[:, :CB] = y2[0:KV] + y2[KV:]
    away[:, CB:] = square


def core_sum_kernel(pos, own, away, *refs):
    outs = refs[-4:]
    for d, out in enumerate(outs):
        at = pl.ds(pl.multiple_of((pos[0] ^ d) * QB, QB), QB)
        out[:KV, :QB] = own[:, at] + away[:, at]
    if away.shape[1] > CB:
        gram = refs[0][...] + away[:, CB:]
        for ref in outs:
            ref[:, QB:] = gram
    else:
        for ref in outs:
            ref[KV:, :] = refs[0][...]


def core_add_kernel(own, away, gram, out):
    out[:, :CB] = own[...] + away[:, :CB]
    out[:, CB:] = gram[...] + away[:, CB:]


def eliminate(gram, y):
    row = lax.broadcasted_iota(jnp.int32, (KV, 128), 0)
    columns = [jnp.broadcast_to(gram[:, j : j + 1], (KV, 128)) for j in range(KV)]
    tiles = [y[:, lo : lo + 128] for lo in range(0, y.shape[1], 128)]
    pivots = jnp.zeros((KV, 128), F32)
    for k in range(KV):
        pivot = columns[k][k : k + 1, :]
        ratio = jnp.where(row > k, columns[k] * (1.0 / pivot), 0.0)
        pivots = jnp.where(row == k, pivot, pivots)
        for j in range(k + 1, KV):
            columns[j] = columns[j] - ratio * columns[j][k : k + 1, :]
        tiles = [tile - ratio * tile[k : k + 1, :] for tile in tiles]
    scale = 1.0 / jnp.sqrt(pivots)
    return jnp.concatenate([tile * scale for tile in tiles], axis=1)


def project_first_kernel(pos, weight_log, q0, q1, q2, q3, out, weight_own, log_degree):
    y = (q0[:KV] + q1[:KV]) + (q2[:KV] + q3[:KV])
    p = y * weight_log[0:1, :]
    for n in range(16):
        out[n] = p
    for d, ref in zip((0, 2, 1, 3), (q0, q1, q2, q3)):
        at = pl.ds(pl.multiple_of((pos[0] ^ d) * QB, QB), QB)
        weight_own[:, at] = ref[KV : KV + 1, :]
        log_degree[:, at] = ref[KV + 1 : KV + 2, :]


def project_kernel(weight_log, q0, q1, q2, q3, out):
    total = (q0[...] + q1[...]) + (q2[...] + q3[...])
    p = eliminate(total[:, QB:], total[:, :QB]) * weight_log[0:1, :]
    for n in range(16):
        out[n] = p


def last_kernel(weight_own, q0, q1, q2, q3, proj, grams):
    total = (q0[...] + q1[...]) + (q2[...] + q3[...])
    y = eliminate(total[:, CB:], total[:, :CB])
    p = y * weight_own[...]
    proj[...] = p
    gram = lax.dot_general(p, p, NT, precision=lax.Precision.HIGHEST, preferred_element_type=F32)
    gram = jnp.concatenate([gram[k : k + 1] for k in range(KV)], axis=1)
    for n in range(32):
        grams[n] = gram


def finish_kernel(proj, grams, log_in, out, log_degree):
    log_degree[...] = log_in[...]
    terms = [grams[n] for n in range(32)]
    while len(terms) > 1:
        terms = [a + b for a, b in zip(terms[::2], terms[1::2])]
    wide = terms[0]
    gram = jnp.concatenate([wide[:, k * KV : (k + 1) * KV] for k in range(KV)], axis=0)
    gram = jnp.concatenate([gram, jnp.zeros((KV, 128 - KV), F32)], axis=1)
    out[...] = eliminate(gram, proj[...]) * math.sqrt(NTOT)


def device_number(x, z, y, c):
    return ((x * 4 + z) * 4 + y) * 2 + c


def shift(v, source):
    pairs = [
        (device_number(*source(x, z, y, c)), device_number(x, z, y, c))
        for x in range(4)
        for z in range(4)
        for y in range(4)
        for c in range(2)
    ]
    return lax.ppermute(v, ("x", "z", "y", "c"), pairs)


def from_line(v, d, second=False):
    def source(x, z, y, c):
        along_y = (c == 0) != second
        return (x, z, y ^ d, c) if along_y else (x, z ^ d, y, c)

    return shift(v, source)


def from_x(v, d):
    return shift(v, lambda x, z, y, c: (x ^ d, z, y, c))


def from_core(v):
    return shift(v, lambda x, z, y, c: (x, z, y, 1 - c))


def body(frames, width_class, start):
    x, z, y, c = (lax.axis_index(a) for a in ("x", "z", "y", "c"))
    second, first = jnp.arange(16, dtype=jnp.int32) // 4, jnp.arange(16, dtype=jnp.int32) % 4
    piece_y = y ^ jnp.where(c == 0, first, second)
    piece_z = z ^ jnp.where(c == 0, second, first)
    pos = jnp.concatenate([jnp.stack([x, c]), piece_y * 4 + piece_z]).astype(jnp.int32)

    classes = width_class.reshape(8, 128)
    piece, mine = call(
        pack_kernel,
        "pack",
        [sds((PROWS, F), BF16), vmem((CB + 16, F), BF16)],
        (pos, *(pltpu.with_memory_space_constraint(a, pltpu.HBM) for a in (frames, classes, start))),
        scratch=[
            pltpu.VMEM((KV, QB), F32),
            pltpu.VMEM((8, 128), jnp.int32),
            pltpu.SemaphoreType.DMA((4,)),
        ],
        far=(1, 2, 3),
    )
    line = [piece] + [from_line(piece, d) for d in (1, 3, 2)]
    shapes = [sds((CB, 2 * F), BF16), sds((1, CB))]
    own_side = call(side_kernel, "own_side", shapes, (keep(mine),), flops=CB * 4000)
    sides = own_side + call(
        side_kernel, "other_side", shapes, (from_core(keep(mine)),), flops=CB * 4000
    )
    line = call(
        stack_kernel, "stack", sds((4, PROWS, F), BF16), (*line, own_side[1])
    )
    groups = [line] + [from_line(line, d, True) for d in (1, 2, 3)]
    ks, sums = [None] * 4, ()
    for step in ((0,), (1,), (2,), (3,)):
        last = step == (3,)
        *made, total = call(
            functools.partial(rows_kernel, len(step), step == (0,), last),
            f"rows{step[0]}",
            [vmem((4 * QB, NJ), BF16)] * len(step) + [sds((128, 1, QB) if last else (8, NJ))],
            (pos, *(groups[g] for g in step), *sides, *sums),
            flops=len(step) * 4 * QB * NJ * 1024,
        )
        sums = (total,)
        for g, k in zip(step, made):
            ks[g] = k

    def tile():
        return [keep(k) for k in ks]

    everyone = ("y", "z", "x", "c")
    dens_i, table = call(
        degree_kernel,
        "degree",
        [sds((1, NI)), sds((128, 1, QB))],
        (pos, *tile(), lax.all_to_all(sums[0], everyone, 0, 0)),
    )
    vec, weight_i, weight_log, away = call(
        first_kernel,
        "first",
        [sds((KV, NI), BF16), sds((1, NI)), sds((8, QB)), sds((KV, CB))],
        (pos, *tile(), *groups, dens_i, lax.all_to_all(table, everyone, 0, 0)),
        scratch=[pltpu.VMEM((1, NI), F32)],
    )
    flops = 2 * NI * CB * 256

    def own_half(iteration):
        return call(own_kernel, f"own{iteration}", sds((KV, CB)), (*tile(), vec), flops=flops)

    for iteration in range(1, ITERS):
        shape = (KV + 8, QB) if iteration == 1 else (KV, QB + 128)
        quarters = call(
            core_sum_kernel,
            f"core_sum{iteration}",
            [sds(shape)] * 4,
            (pos, own_half(iteration), from_core(away), weight_log if iteration == 1 else square),
        )
        quarters = [quarters[0]] + [from_x(quarters[d], d) for d in (2, 1, 3)]
        if iteration == 1:
            pieces, weight_own, log_degree = call(
                project_first_kernel,
                "project1",
                [sds((16, KV, QB)), sds((1, CB)), sds((1, CB))],
                (pos, weight_log, *quarters),
            )
        else:
            pieces = call(
                project_kernel,
                f"project{iteration}",
                sds((16, KV, QB)),
                (weight_log, *quarters),
            )
        pieces = lax.all_to_all(pieces, ("y", "z"), 0, 0)
        vec, square, away = call(
            next_kernel,
            f"next{iteration}",
            [sds((2 * KV, NI), BF16), sds((KV, 128)), sds((KV, CB + 128))],
            (pos, *tile(), weight_i, pieces),
            scratch=[pltpu.VMEM((3 * KV, NI), BF16)],
        )
    total = call(
        core_add_kernel,
        "core_add",
        sds((KV, CB + 128)),
        (own_half(ITERS), from_core(away), square),
    )
    totals = [total] + [from_x(total, d) for d in (1, 3, 2)]
    proj, grams = call(
        last_kernel, "last", [sds((KV, CB)), sds((32, 1, KV * KV))], (weight_own, *totals)
    )
    grams = lax.all_to_all(grams, ("z", "y", "c"), 0, 0)
    embedding, log_degree = call(
        finish_kernel, "finish", [sds((KV, CB)), sds((1, CB))], (proj, grams, log_degree)
    )
    return embedding, log_degree.reshape(CB)


def solution(mesh):
    grid = Mesh(mesh.devices.reshape(4, 4, 4, 2), ("x", "z", "y", "c"))
    col = ("z", "y", "c")
    in_specs = (P(col, None), P(col), P(None, col))
    out_specs = (P(None, col), P(col))
    return jax.shard_map(body, mesh=grid, in_specs=in_specs, out_specs=out_specs, check_vma=False)
```
